128 devices in a mesh: gy: 32 (over x, y, core), gz: 4 (over z).
Axes of the slice: x: 4, y: 4, z: 4, core: 2. Of those that a mesh axis runs over, the one named last changes fastest.
Arguments:
- image: bfloat16 [128, 768, 128], P('gz', 'gy'), may hold values from -6 to 6
- labels: int32 [128, 768, 128], P('gz', 'gy'), may hold values from 0 to 2047
- brick_blocks: int32 [4, 32, 16], P('gz', 'gy'), may hold values from 0 to 127, as said below
- block_owner: int32 [128], replicated, may hold values from 0 to 31, as said below
Outputs:
- likeness: bfloat16 [128, 768, 128], P('gz', 'gy')
- label_features: float32 [128, 64, 128], P('gy', 'gz')
The draws below stay inside these ranges and needn't reach their ends.
Inputs may be any that keep to these rules, and one draw needn't show every extreme that they name: `block_owner`: each index of gy owns exactly 4 blocks. `brick_blocks`: each brick lists 16 distinct blocks, no two of them with the same owner; one owner is listed by every brick.
All inputs are finite; a program needn't handle non-finite values.
Results may differ from the reference program's by a relative error of at most 0.009.
Values may be sent and summed in bfloat16 or wider, within the bound.
No kernel may reach another device: no remote copies, remote signals or barrier semaphores. Data moves between devices by JAX's collectives and lax.ppermute only.
A program may use at most 128 MiB of HBM per device.

```python
import math
import jax
import jax.numpy as jnp
from jax import lax

NX = 128
CY = 24
SLAB = 128
LBL = 128
FEAT = 64
BLK_DEV = 4
KB = 16
NY = 768
NBLK = 128
NLAB = 16384
N_GY = 32
N_GZ = 4


def block_layout(key):
    shuffled = jax.random.permutation(jax.random.fold_in(key, 11), NBLK).astype(jnp.int32)
    owner_of = (shuffled // BLK_DEV).astype(jnp.int32)
    owned_order = jnp.argsort(shuffled).astype(jnp.int32)
    return (owner_of, owned_order)


def draw_block_owner(key, part):
    return block_layout(key)[0]


def draw_brick_blocks(key, part):
    owner_of, owned_order = block_layout(key)
    hot_owner = jax.random.randint(jax.random.fold_in(key, 12), (), 0, N_GY).astype(jnp.int32)
    brick_keys = jax.random.split(jax.random.fold_in(key, 13), N_GZ * N_GY)

    def pick_blocks(brick_key):
        first_key, second_key, tertiary_key = jax.random.split(brick_key, 3)
        others = jax.random.permutation(first_key, N_GY - 1)[:KB - 1].astype(jnp.int32)
        others = jnp.where(others >= hot_owner, others + 1, others)
        owners = jnp.concatenate([hot_owner[None], others]).astype(jnp.int32)
        owners = owners[jax.random.permutation(tertiary_key, KB)]
        offset_pick = jax.random.randint(second_key, (KB,), 0, BLK_DEV).astype(jnp.int32)
        return owned_order[owners * BLK_DEV + offset_pick]
    return jax.vmap(pick_blocks)(brick_keys).reshape(N_GZ, N_GY, KB).astype(jnp.int32)


def with_ends(entries, own_key, low, largest):
    dims = entries.shape
    spot = [jax.random.randint(jax.random.fold_in(own_key, axis), (), 0, dims[axis]) for axis in range(len(dims))]
    entries = entries.at[tuple(spot)].set(low)
    longest = dims.index(max(dims))
    spot[longest] = (spot[longest] + 1) % dims[longest]
    return entries.at[tuple(spot)].set(largest)


def block_scale(key, shape, cuts, low, top_value):
    gain = 1.0
    for dim, shards_of in cuts:
        steps = jax.random.uniform(jax.random.fold_in(jax.random.fold_in(key, 6), dim), (shards_of,), jnp.float32, low / len(cuts), top_value / len(cuts))
        gain = gain * jnp.repeat(jnp.exp(steps), shape[dim] // shards_of).reshape((-1,) + (1,) * (len(shape) - 1 - dim))
    return gain


def bell_draw(stream_key, shape, deviation, bound, pieces=(), kind=jnp.bfloat16):
    result = deviation * jax.random.normal(stream_key, shape, jnp.float32)
    if pieces:
        result = result * block_scale(stream_key, shape, pieces, -0.22, 0.18)
    return jnp.clip(result, -bound, bound).astype(kind)


def setup_inputs(seed: int = 0) -> dict:
    key_of = jax.random.split(jax.random.key(seed), 5)
    return {
        "image": bell_draw(key_of[0], (SLAB, NY, NX), 1.0, 6.0, ((0, 4), (1, 32))),
        "labels": with_ends(jax.random.randint(key_of[1], (SLAB, NY, NX), 0, KB * LBL), jax.random.fold_in(key_of[1], 1), 0, (KB * LBL) - 1).astype(jnp.int32),
        "brick_blocks": draw_brick_blocks(jax.random.fold_in(key_of[4], 71), 0),
        "block_owner": draw_block_owner(jax.random.fold_in(key_of[4], 71), 0),
    }


CENTERS = (-1.5, -0.5, 0.5, 1.5)


def kernel_set(sigma_val):
    radius = 3 * sigma_val
    offsets = [float(step) for step in range(-radius, radius + 1)]
    smooth = [math.exp(-step * step / (2.0 * sigma_val ** 2)) for step in offsets]
    weight_total = sum(smooth)
    smooth = [value / weight_total for value in smooth]
    first_order = [step / sigma_val ** 2 * value for step, value in zip(offsets, smooth)]
    second = [(step * step / sigma_val ** 4 - 1.0 / sigma_val ** 2) * value for step, value in zip(offsets, smooth)]
    return radius, [smooth, first_order, second]


def along(volume_in, weights, dim_index, length_out):
    summed = weights[0] * lax.slice_in_dim(volume_in, 0, length_out, axis=dim_index)
    for tap_index in range(1, len(weights)):
        summed = summed + weights[tap_index] * lax.slice_in_dim(volume_in, tap_index, tap_index + length_out, axis=dim_index)
    return summed


def plane_pass(extended, sigma_val):
    radius, filters = kernel_set(sigma_val)
    inner_width = extended.shape[2]
    inner_rows = extended.shape[1] - 2 * radius
    padded = jnp.pad(extended, ((0, 0), (0, 0), (radius, radius)))
    along_x = [along(padded, filters[sorted_along_width], 2, inner_width) for sorted_along_width in range(3)]
    combos = ((2, 0), (0, 2), (0, 0), (1, 1), (1, 0), (0, 1))
    return jnp.stack([along(along_x[sorted_along_width], filters[order_y], 1, inner_rows) for sorted_along_width, order_y in combos])


def depth_pass(stacked, sigma_val):
    radius, filters = kernel_set(sigma_val)
    inner_depth = stacked.shape[1] - 2 * radius
    orders = (0, 0, 2, 0, 1, 1)
    return jnp.stack([along(stacked[channel], filters[sorted_along_depth], 0, inner_depth) for channel, sorted_along_depth in enumerate(orders)])


def throat_channels(hessian, sigma_val):
    scaled = hessian * (4.0 * sigma_val ** 3.5)
    trace_sum = scaled[0] + scaled[1] + scaled[2]
    frobenius = scaled[0] ** 2 + scaled[1] ** 2 + scaled[2] ** 2 + 2.0 * (scaled[3] ** 2 + scaled[4] ** 2 + scaled[5] ** 2)
    minors = 0.5 * (trace_sum * trace_sum - frobenius)
    tube_value = jnp.maximum(-trace_sum, 0.0) * jnp.maximum(minors, 0.0) / (frobenius + 0.25)
    return jnp.concatenate([scaled, minors[None], tube_value[None]]), tube_value


def feature_rows(feature_channels, volume):
    intensity_bands = jnp.stack([jnp.exp(-(volume - center) ** 2) for center in CENTERS])
    mixed = feature_channels[:, None] * intensity_bands[None]
    return mixed.reshape(feature_channels.shape[0] * len(CENTERS), -1).astype(jnp.bfloat16)


def reference(image, labels, brick_blocks, block_owner):
    volume = image.astype(jnp.float32)
    padded = jnp.pad(volume, ((12, 12), (12, 12), (0, 0)))
    rows_z = jnp.repeat(brick_blocks, SLAB // N_GZ, axis=0)
    kinds = jnp.arange(KB, dtype=jnp.int32)

    def column(running, brick_row):
        start = (brick_row * CY).astype(jnp.int32)
        window = lax.dynamic_slice_in_dim(padded, start, CY + 24, 1)
        channel_list = []
        tube_list = []
        for sigma_val in (2, 4):
            radius = 3 * sigma_val
            inner = window[12 - radius: 12 + SLAB + radius, 12 - radius: 12 + CY + radius]
            hessian = depth_pass(plane_pass(inner, sigma_val), sigma_val)
            feature_channels, tube_value = throat_channels(hessian, sigma_val)
            channel_list.append(feature_channels)
            tube_list.append(tube_value)
        center_volume = lax.dynamic_slice_in_dim(volume, start, CY, 1)
        feats = feature_rows(jnp.concatenate(channel_list), center_volume)
        local = lax.dynamic_slice_in_dim(labels, start, CY, 1)
        listed = lax.dynamic_index_in_dim(rows_z, brick_row, 1, keepdims=False)
        slot_kind = local // LBL
        block_id = jnp.sum(jnp.where(slot_kind[..., None] == kinds, listed[:, None, None, :], 0), axis=-1).astype(jnp.int32)
        label_id = (block_id * LBL + local % LBL).astype(jnp.int32)
        running = running + jax.ops.segment_sum(feats.astype(jnp.float32).T, label_id.reshape(-1), num_segments=NLAB)
        return running, jnp.maximum(tube_list[0], tube_list[1]).astype(jnp.bfloat16)

    sums, columns = lax.scan(column, jnp.zeros((NLAB, FEAT), jnp.float32), jnp.arange(N_GY, dtype=jnp.int32))
    likeness = columns.transpose(1, 0, 2, 3).reshape(SLAB, NY, NX)
    block_index = jnp.arange(NBLK, dtype=jnp.int32)
    earlier = (block_index[None, :] < block_index[:, None]) & (block_owner[None, :] == block_owner[:, None])
    owner_rank = jnp.sum(earlier.astype(jnp.int32), axis=1)
    slot_pos = (block_owner * BLK_DEV + owner_rank).astype(jnp.int32)
    per_block = sums.reshape(NBLK, LBL, FEAT).transpose(0, 2, 1)
    arranged = jnp.zeros_like(per_block).at[slot_pos].set(per_block)
    return likeness, arranged
```

```python
import math

import jax
import jax.numpy as jnp
import ml_dtypes
import numpy as np
from jax import lax
from jax.experimental import pallas as pl
from jax.experimental.pallas import tpu as pltpu
from jax.sharding import PartitionSpec as P

LBL = 128
FEAT = 64
HALO = 12
ZC = 8
SIGMAS = (2, 4)
CENTERS = (-1.5, -0.5, 0.5, 1.5)
ORDERS = ((2, 0, 0), (0, 2, 0), (0, 0, 2), (1, 1, 0), (1, 0, 1), (0, 1, 1))
HI = 8
LO = 256
SEND = 24
F32, BF16 = jnp.float32, jnp.bfloat16


def kernel_set(sigma_val):
    radius = 3 * sigma_val
    offsets = [float(step) for step in range(-radius, radius + 1)]
    smooth = [math.exp(-step * step / (2.0 * sigma_val**2)) for step in offsets]
    weight_total = sum(smooth)
    smooth = [value / weight_total for value in smooth]
    first_order = [step / sigma_val**2 * value for step, value in zip(offsets, smooth)]
    second = [
        (step * step / sigma_val**4 - 1.0 / sigma_val**2) * value
        for step, value in zip(offsets, smooth)
    ]
    return (radius, [smooth, first_order, second])


def banded(weights, radius, rows, columns, offset):
    matrix = np.zeros((rows, columns))
    for row in range(rows):
        for tap, weight in enumerate(weights):
            column = row + offset + tap - radius
            if 0 <= column < columns:
                matrix[row, column] = weight
    return matrix


def two_parts(matrix):
    high = matrix.astype(np.float32).astype(ml_dtypes.bfloat16)
    low = (matrix - high.astype(np.float64)).astype(np.float32).astype(ml_dtypes.bfloat16)
    return (high, low)


def filter_matrices(rows_y, width):
    along_z, along_y, along_x = ([], [], [])
    for sigma_val in SIGMAS:
        radius, filters = kernel_set(sigma_val)
        y_rows = []
        for order in range(3):
            z_matrix = banded(filters[order], radius, ZC, ZC + 2 * HALO, HALO)
            along_z.append(np.kron(z_matrix, np.eye(8)))
            y_rows.append(banded(filters[order], radius, rows_y, rows_y + 2 * HALO, HALO))
            x_matrix = banded(filters[order], radius, width, width, 0).T
            high, low = two_parts(x_matrix * (4.0 * sigma_val**3.5))
            along_x.append(np.concatenate([high, high, low], axis=0))
        y_matrix = np.concatenate(y_rows)
        y_matrix = np.pad(y_matrix, ((0, -y_matrix.shape[0] % 16), (0, 0)))
        high, low = two_parts(y_matrix)
        along_y.append(np.concatenate([high, high, low], axis=1))
    z_high, z_low = two_parts(np.concatenate(along_z))
    return (np.stack([z_high, z_low]), np.stack(along_y), np.stack(along_x))


def split(value):
    high = value.astype(BF16)
    return (high, (value - high.astype(F32)).astype(BF16))


def throat_kernel(
    owner_ref, rank_ref, ext_ref, labels_ref, wz_ref, wy_ref, wx_ref,
    like_ref, send_ref,
    z_high, z_low, y_out, channels, bands, acc, turned,
):
    chunk = pl.program_id(0)
    rows_y = labels_ref.shape[1]
    deep = rows_y + 2 * HALO
    rows = ZC * rows_y
    width = labels_ref.shape[2]
    z_start = chunk * ZC

    for pair in range(deep // 16):
        tiles = [
            ext_ref[pl.ds(z_start, ZC + 2 * HALO), pl.ds(16 * pair + 8 * half, 8), :]
            .reshape((ZC + 2 * HALO) * 8, width)
            .astype(BF16)
            for half in range(2)
        ]
        grey = jnp.concatenate(tiles, axis=1)
        out = jnp.dot(wz_ref[0], grey, preferred_element_type=F32) + jnp.dot(
            wz_ref[1], grey, preferred_element_type=F32
        )
        out = out.reshape(6 * ZC, 8, 2 * width)
        out = jnp.concatenate([out[:, :, :width], out[:, :, width:]], axis=1)
        high, low = split(out)
        z_high[:, pl.ds(16 * pair, 16), :] = high
        z_low[:, pl.ds(16 * pair, 16), :] = low

    for scale in range(2):
        for order_z in range(3):
            for pair in range(ZC // 2):
                columns = []
                for half in range(2):
                    index = (scale * 3 + order_z) * ZC + 2 * pair + half
                    columns.append(
                        jnp.concatenate([z_high[index], z_low[index], z_high[index]], axis=0)
                    )
                deep_rows = jnp.concatenate(columns, axis=1)
                count = wy_ref.shape[1] if order_z == 0 else (48 if order_z == 1 else 32)
                out = jnp.dot(
                    wy_ref[scale, :count, :], deep_rows, preferred_element_type=F32
                )
                for order_y in range(3 - order_z):
                    component = [
                        i for i, o in enumerate(ORDERS) if o[1:] == (order_y, order_z)
                    ][0]
                    for half in range(2):
                        y_out[
                            scale * 6 + component, pl.ds((2 * pair + half) * rows_y, rows_y), :
                        ] = out[
                            order_y * rows_y : (order_y + 1) * rows_y,
                            half * width : (half + 1) * width,
                        ]

    tubes = []
    for scale in range(2):
        hessian = []
        for component, order in enumerate(ORDERS):
            high, low = split(y_out[scale * 6 + component])
            hessian.append(
                jnp.dot(
                    jnp.concatenate([high, low, high], axis=1),
                    wx_ref[scale * 3 + order[0]],
                    preferred_element_type=F32,
                )
            )
        xx, yy, zz, xy, xz, yz = hessian
        trace = xx + yy + zz
        frob = xx * xx + yy * yy + zz * zz + 2.0 * (xy * xy + xz * xz + yz * yz)
        minors = 0.5 * (trace * trace - frob)
        tube = jnp.maximum(-trace, 0.0) * jnp.maximum(minors, 0.0) / (frob + 0.25)
        tubes.append(tube)
        for index, value in enumerate(hessian + [minors, tube]):
            channels[pl.ds((scale * 8 + index) * rows, rows), :] = value
    like = jnp.maximum(tubes[0], tubes[1])
    like_ref[...] = like.reshape(ZC, rows_y, width).astype(BF16)

    volume = ext_ref[pl.ds(z_start + HALO, ZC), pl.ds(HALO, rows_y), :].astype(F32)
    volume = volume.reshape(rows, width)
    for index, center in enumerate(CENTERS):
        bands[pl.ds(index * rows, rows), :] = jnp.exp(-((volume - center) ** 2))

    @pl.when(chunk == 0)
    def _():
        acc[...] = jnp.zeros_like(acc)

    group = 8
    low_ids = lax.broadcasted_iota(jnp.int32, (LO, width), 0).astype(F32).astype(BF16)

    def step(index, carry):
        row0 = index * group
        plane = row0 // rows_y
        first = row0 - plane * rows_y
        left, right = ([], [])
        marks = labels_ref[plane, pl.ds(pl.multiple_of(first, 8), 8), :]
        mark_high = (marks >> 8).astype(F32)
        mark_low = (marks & 255).astype(F32)
        for row in range(group):
            feats = []
            for scale in range(2):
                base = channels[pl.ds(scale * 8 * rows + row0 + row, 8, stride=rows), :]
                for band in range(4):
                    gain = bands[pl.ds(band * rows + row0 + row, 1), :]
                    feats.append(base * gain)
            feats = jnp.concatenate(feats, axis=0).astype(BF16)
            high_of = jnp.broadcast_to(mark_high[row : row + 1], (FEAT, width)).astype(BF16)
            low_of = jnp.broadcast_to(mark_low[row : row + 1], (LO, width)).astype(BF16)
            zero = jnp.zeros_like(feats)
            left.append(
                jnp.concatenate(
                    [jnp.where(high_of == jnp.asarray(h, BF16), feats, zero) for h in range(HI)],
                    axis=0,
                )
            )
            right.append(
                jnp.where(low_of == low_ids, jnp.asarray(1, BF16), jnp.asarray(0, BF16))
            )
        acc[...] += lax.dot_general(
            jnp.concatenate(left, axis=1),
            jnp.concatenate(right, axis=1),
            (((1,), (1,)), ((), ())),
            preferred_element_type=F32,
        )
        return carry

    lax.fori_loop(0, rows // group, step, 0)

    @pl.when(chunk == pl.num_programs(0) - 1)
    def _():
        send_ref[...] = jnp.zeros_like(send_ref)
        for slot in range(owner_ref.shape[0]):
            owner = owner_ref[slot]
            rank = rank_ref[slot].astype(F32)
            for scale in range(2):
                for band in range(4):
                    turned[pl.ds(32 * scale + band, 8, stride=4), :] = acc[
                        pl.ds((slot // 2) * FEAT + 32 * scale + 8 * band, 8),
                        pl.ds((slot % 2) * LBL, LBL),
                    ]
            for quarter in range(4):
                send_ref[owner, quarter, pl.ds(0, 16), :] = turned[
                    pl.ds(16 * quarter, 16), :
                ].astype(BF16)
                send_ref[owner, quarter, pl.ds(16, 8), :] = jnp.full((8, LBL), rank, F32).astype(
                    BF16
                )


def sum_kernel(got_ref, out_ref):
    sources = got_ref.shape[0]

    def step(source, totals):
        block = got_ref[source].astype(F32)
        data, rank = (block[:16], jnp.concatenate([block[16:], block[16:]], axis=0))
        return tuple(
            total + jnp.where(rank == float(index), data, 0.0) for index, total in enumerate(totals)
        )

    totals = lax.fori_loop(
        0, sources, step, tuple(jnp.zeros(out_ref.shape[1:], F32) for _ in range(out_ref.shape[0]))
    )
    for index, total in enumerate(totals):
        out_ref[index] = total


def extended_2(shard, sides, width):
    for axis, dim in sides:
        size, length = (lax.axis_size(axis), shard.shape[dim])
        up = [(i, (i + 1) % size) for i in range(size - 1)]
        down = [(j, i) for i, j in up]
        last = lax.slice_in_dim(shard, length - width, length, axis=dim)
        leading = lax.slice_in_dim(shard, 0, width, axis=dim)
        before = lax.ppermute(last, axis, up)
        after = lax.ppermute(leading, axis, down)
        shard = jnp.concatenate([before, shard, after], axis=dim)
    return shard


def throat_sums(ext, labels, owners, ranks, groups, quarters):
    slab_z, rows_y, width = labels.shape
    matrices = filter_matrices(rows_y, width)
    rows = ZC * rows_y
    deep = rows_y + 2 * HALO
    whole = lambda array: pl.BlockSpec(array.shape, lambda i, *_: (0,) * array.ndim)
    return pl.pallas_call(
        throat_kernel,
        out_shape=(
            jax.ShapeDtypeStruct(labels.shape, BF16),
            jax.ShapeDtypeStruct((groups, quarters, SEND, LBL), BF16),
        ),
        grid_spec=pltpu.PrefetchScalarGridSpec(
            num_scalar_prefetch=2,
            grid=(slab_z // ZC,),
            in_specs=[
                whole(ext),
                pl.BlockSpec((ZC, rows_y, width), lambda i, *_: (i, 0, 0)),
                *[whole(matrix) for matrix in matrices],
            ],
            out_specs=(
                pl.BlockSpec((ZC, rows_y, width), lambda i, *_: (i, 0, 0)),
                pl.BlockSpec((groups, quarters, SEND, LBL), lambda i, *_: (0, 0, 0, 0)),
            ),
            scratch_shapes=[
                pltpu.VMEM((6 * ZC, deep, width), BF16),
                pltpu.VMEM((6 * ZC, deep, width), BF16),
                pltpu.VMEM((12, rows, width), F32),
                pltpu.VMEM((16 * rows, width), F32),
                pltpu.VMEM((4 * rows, width), F32),
                pltpu.VMEM((HI * FEAT, LO), F32),
                pltpu.VMEM((FEAT, LBL), F32),
            ],
        ),
        compiler_params=pltpu.CompilerParams(vmem_limit_bytes=48 * 1024 * 1024),
    )(owners, ranks, ext, labels, *matrices)


def local(image, labels, brick_blocks, block_owner):
    groups = lax.axis_size("gy")
    quarters = lax.axis_size("gz")
    listed_count = brick_blocks.shape[-1]
    total_blocks = block_owner.shape[0]
    blk_dev = total_blocks // groups
    block_index = jnp.arange(total_blocks, dtype=jnp.int32)
    earlier = (block_index[None, :] < block_index[:, None]) & (
        block_owner[None, :] == block_owner[:, None]
    )
    owner_rank = jnp.sum(earlier.astype(jnp.int32), axis=1)
    listed_ids = brick_blocks.reshape(listed_count)
    listed = (listed_ids[:, None] == block_index[None, :]).astype(jnp.int32)
    owners = jnp.sum(listed * block_owner[None, :], axis=1)
    ranks = jnp.sum(listed * owner_rank[None, :], axis=1)

    ext = extended_2(image, (("gy", 1), ("gz", 0)), HALO).astype(F32)
    likeness, message = throat_sums(ext, labels, owners, ranks, groups, quarters)
    message = message.reshape(groups * quarters, SEND, LBL)
    got = lax.all_to_all(message, ("gy", "gz"), 0, 0, tiled=True)
    label_features = pl.pallas_call(
        sum_kernel,
        out_shape=jax.ShapeDtypeStruct((blk_dev, FEAT // quarters, LBL), F32),
    )(got)
    return (likeness, label_features)


def solution(mesh):
    placed = (P("gz", "gy", None), P("gz", "gy", None), P("gz", "gy", None), P())
    return jax.shard_map(
        local,
        mesh=mesh,
        in_specs=placed,
        out_specs=(P("gz", "gy", None), P("gy", "gz", None)),
        check_vma=False,
    )
```

```python
import math

import jax
import jax.numpy as jnp
import ml_dtypes
import numpy as np
from jax import lax
from jax.experimental import pallas as pl
from jax.experimental.pallas import tpu as pltpu
from jax.sharding import PartitionSpec as P

LBL = 128
FEAT = 64
HALO = 12
ZC = 4
PLANES = 4
SIGMAS = (2, 4)
CENTERS = (-1.5, -0.5, 0.5, 1.5)
ORDERS = ((2, 0, 0), (0, 2, 0), (0, 0, 2), (1, 1, 0), (1, 0, 1), (0, 1, 1))
HI = 8
LO = 256
SEND = 24
F32, BF16 = jnp.float32, jnp.bfloat16


def kernel_set(sigma_val):
    radius = 3 * sigma_val
    offsets = [float(step) for step in range(-radius, radius + 1)]
    smooth = [math.exp(-step * step / (2.0 * sigma_val**2)) for step in offsets]
    weight_total = sum(smooth)
    smooth = [value / weight_total for value in smooth]
    first_order = [step / sigma_val**2 * value for step, value in zip(offsets, smooth)]
    second = [
        (step * step / sigma_val**4 - 1.0 / sigma_val**2) * value
        for step, value in zip(offsets, smooth)
    ]
    return (radius, [smooth, first_order, second])


def banded(weights, radius, rows, columns, offset):
    matrix = np.zeros((rows, columns))
    for row in range(rows):
        for tap, weight in enumerate(weights):
            column = row + offset + tap - radius
            if 0 <= column < columns:
                matrix[row, column] = weight
    return matrix


def two_parts(matrix):
    high = matrix.astype(np.float32).astype(ml_dtypes.bfloat16)
    low = (matrix - high.astype(np.float64)).astype(np.float32).astype(ml_dtypes.bfloat16)
    return (high, low)


def filter_matrices(rows_y, width):
    along_z, along_y, along_x = ([], [], [])
    for sigma_val in SIGMAS:
        radius, filters = kernel_set(sigma_val)
        y_rows = []
        for order in range(3):
            z_matrix = banded(filters[order], radius, ZC, ZC + 2 * HALO, HALO)
            along_z.append(np.kron(z_matrix, np.eye(8)))
            y_rows.append(banded(filters[order], radius, rows_y, rows_y + 2 * HALO, HALO))
            x_matrix = banded(filters[order], radius, width, width, 0).T
            high, low = two_parts(x_matrix * (4.0 * sigma_val**3.5))
            along_x.append(np.concatenate([high, high, low], axis=0))
        y_matrix = np.concatenate(y_rows)
        y_matrix = np.pad(y_matrix, ((0, -y_matrix.shape[0] % 16), (0, 0)))
        high, low = two_parts(y_matrix)
        along_y.append(np.concatenate([high, high, low], axis=1))
    z_high, z_low = two_parts(np.concatenate(along_z))
    return (np.stack([z_high, z_low]), np.stack(along_y), np.stack(along_x))


def split(value):
    high = value.astype(BF16)
    return (high, (value - high.astype(F32)).astype(BF16))


def filters_of(z_start, ext, wz_ref, wy_ref, wx_ref, z_high, z_low, y_out, channels, bands, like_ref):
    rows_y, width = like_ref.shape[1:]
    deep = rows_y + 2 * HALO
    rows = ZC * rows_y

    for pair in range(deep // 16):
        tiles = [
            ext[pl.ds(z_start, ZC + 2 * HALO), pl.ds(16 * pair + 8 * half, 8), :]
            .reshape((ZC + 2 * HALO) * 8, width)
            .astype(BF16)
            for half in range(2)
        ]
        grey = jnp.concatenate(tiles, axis=1)
        out = jnp.dot(wz_ref[0], grey, preferred_element_type=F32) + jnp.dot(
            wz_ref[1], grey, preferred_element_type=F32
        )
        out = out.reshape(6 * ZC, 8, 2 * width)
        out = jnp.concatenate([out[:, :, :width], out[:, :, width:]], axis=1)
        high, low = split(out)
        z_high[:, pl.ds(16 * pair, 16), :] = high
        z_low[:, pl.ds(16 * pair, 16), :] = low

    for scale in range(2):
        for order_z in range(3):
            for pair in range(ZC // 2):
                columns = []
                for half in range(2):
                    index = (scale * 3 + order_z) * ZC + 2 * pair + half
                    columns.append(
                        jnp.concatenate([z_high[index], z_low[index], z_high[index]], axis=0)
                    )
                deep_rows = jnp.concatenate(columns, axis=1)
                count = wy_ref.shape[1] if order_z == 0 else (48 if order_z == 1 else 32)
                out = jnp.dot(
                    wy_ref[scale, :count, :], deep_rows, preferred_element_type=F32
                )
                for order_y in range(3 - order_z):
                    component = [
                        i for i, o in enumerate(ORDERS) if o[1:] == (order_y, order_z)
                    ][0]
                    for half in range(2):
                        y_out[
                            scale * 6 + component, pl.ds((2 * pair + half) * rows_y, rows_y), :
                        ] = out[
                            order_y * rows_y : (order_y + 1) * rows_y,
                            half * width : (half + 1) * width,
                        ]

    tubes = []
    for scale in range(2):
        hessian = []
        for component, order in enumerate(ORDERS):
            high, low = split(y_out[scale * 6 + component])
            hessian.append(
                jnp.dot(
                    jnp.concatenate([high, low, high], axis=1),
                    wx_ref[scale * 3 + order[0]],
                    preferred_element_type=F32,
                )
            )
        xx, yy, zz, xy, xz, yz = hessian
        trace = xx + yy + zz
        frob = xx * xx + yy * yy + zz * zz + 2.0 * (xy * xy + xz * xz + yz * yz)
        minors = 0.5 * (trace * trace - frob)
        tube = jnp.maximum(-trace, 0.0) * jnp.maximum(minors, 0.0) / (frob + 0.25)
        tubes.append(tube)
        for index, value in enumerate(hessian + [minors, tube]):
            channels[pl.ds((scale * 8 + index) * rows, rows), :] = value
    like = jnp.maximum(tubes[0], tubes[1])
    like_ref[pl.ds(z_start, ZC)] = like.reshape(ZC, rows_y, width).astype(BF16)

    volume = ext[pl.ds(z_start + HALO, ZC), pl.ds(HALO, rows_y), :].reshape(rows, width)
    for index, center in enumerate(CENTERS):
        bands[pl.ds(index * rows, rows), :] = jnp.exp(-((volume - center) ** 2))


def add_sums(z_start, labels_ref, channels, bands, acc):
    rows_y, width = labels_ref.shape[1:]
    rows = ZC * rows_y
    group = PLANES * rows_y
    low_ids = lax.broadcasted_iota(jnp.int32, (LO, width), 0).astype(F32).astype(BF16)
    for part in range(ZC // PLANES):
        left, right = ([], [])
        marks = labels_ref[pl.ds(z_start + part * PLANES, PLANES)].reshape(group, width)
        mark_high = (marks >> 8).astype(F32)
        mark_low = (marks & 255).astype(F32)
        for row in range(group):
            at = part * group + row
            feats = []
            for scale in range(2):
                base = channels[pl.ds(scale * 8 * rows + at, 8, stride=rows), :]
                for band in range(4):
                    feats.append(base * bands[pl.ds(band * rows + at, 1), :])
            feats = jnp.concatenate(feats, axis=0).astype(BF16)
            high_of = jnp.broadcast_to(mark_high[row : row + 1], (FEAT, width)).astype(BF16)
            low_of = jnp.broadcast_to(mark_low[row : row + 1], (LO, width)).astype(BF16)
            zero = jnp.zeros_like(feats)
            left.append(
                jnp.concatenate(
                    [jnp.where(high_of == jnp.asarray(h, BF16), feats, zero) for h in range(HI)],
                    axis=0,
                )
            )
            right.append(
                jnp.where(low_of == low_ids, jnp.asarray(1, BF16), jnp.asarray(0, BF16))
            )
        acc[...] += lax.dot_general(
            jnp.concatenate(left, axis=1),
            jnp.concatenate(right, axis=1),
            (((1,), (1,)), ((), ())),
            preferred_element_type=F32,
        )


def inner_kernel(
    own_ref, labels_ref, wz_ref, wy_ref, wx_ref,
    like_ref, acc,
    ext, z_high, z_low, y_out, channels_0, channels_1, bands_0, bands_1,
):
    slab_z = labels_ref.shape[0]
    ext[pl.ds(HALO, slab_z)] = own_ref[...].astype(F32)
    acc[...] = jnp.zeros_like(acc)
    buffers = ((channels_0, bands_0), (channels_1, bands_1))
    starts = range(HALO, slab_z - HALO, ZC)
    for index, z_start in enumerate(starts):
        filters_of(
            z_start, ext, wz_ref, wy_ref, wx_ref, z_high, z_low, y_out,
            *buffers[index % 2], like_ref,
        )
        if index:
            add_sums(z_start - ZC, labels_ref, *buffers[(index - 1) % 2], acc)
    add_sums(starts[-1], labels_ref, *buffers[(len(starts) - 1) % 2], acc)


def outer_kernel(
    owner_ref, rank_ref, before_ref, own_ref, after_ref, labels_ref, wz_ref, wy_ref, wx_ref,
    inner_like_ref, inner_acc_ref,
    like_ref, send_ref,
    ext, z_high, z_low, y_out, channels_0, channels_1, bands_0, bands_1, acc, turned,
):
    slab_z = labels_ref.shape[0]
    ext[pl.ds(0, HALO)] = before_ref[...].astype(F32)
    ext[pl.ds(HALO, slab_z)] = own_ref[...].astype(F32)
    ext[pl.ds(HALO + slab_z, HALO)] = after_ref[...].astype(F32)
    acc[...] = inner_acc_ref[...]
    inner = pl.ds(HALO, slab_z - 2 * HALO)
    like_ref[inner] = inner_like_ref[inner]
    half = HALO // ZC
    count = 2 * half

    def start_of(index):
        return index * ZC + jnp.where(index >= half, slab_z - 2 * HALO, 0)

    def filters(index, channels, bands):
        filters_of(
            start_of(index), ext, wz_ref, wy_ref, wx_ref, z_high, z_low, y_out,
            channels, bands, like_ref,
        )

    filters(jnp.int32(0), channels_0, bands_0)

    def step(index, carry):
        first = 2 * index
        filters(first + 1, channels_1, bands_1)
        add_sums(start_of(first), labels_ref, channels_0, bands_0, acc)
        filters(jnp.minimum(first + 2, count - 1), channels_0, bands_0)
        add_sums(start_of(first + 1), labels_ref, channels_1, bands_1, acc)
        return carry

    lax.fori_loop(0, count // 2, step, 0)

    send_ref[...] = jnp.zeros_like(send_ref)
    for slot in range(owner_ref.shape[0]):
        owner = owner_ref[slot]
        rank = rank_ref[slot].astype(F32)
        for scale in range(2):
            for band in range(4):
                turned[pl.ds(32 * scale + band, 8, stride=4), :] = acc[
                    pl.ds((slot // 2) * FEAT + 32 * scale + 8 * band, 8),
                    pl.ds((slot % 2) * LBL, LBL),
                ]
        for quarter in range(4):
            send_ref[owner, quarter, pl.ds(0, 16), :] = turned[pl.ds(16 * quarter, 16), :].astype(
                BF16
            )
            send_ref[owner, quarter, pl.ds(16, 8), :] = jnp.full((8, LBL), rank, F32).astype(BF16)


def sum_kernel(got_ref, out_ref):
    sources = got_ref.shape[0]

    def step(source, totals):
        block = got_ref[source].astype(F32)
        data, rank = (block[:16], jnp.concatenate([block[16:], block[16:]], axis=0))
        return tuple(
            total + jnp.where(rank == float(index), data, 0.0) for index, total in enumerate(totals)
        )

    totals = lax.fori_loop(
        0,
        sources,
        step,
        tuple(jnp.zeros(out_ref.shape[1:], F32) for _ in range(out_ref.shape[0])),
        unroll=8,
    )
    for index, total in enumerate(totals):
        out_ref[index] = total


def extended(shard, axis, dim, width):
    size, length = (lax.axis_size(axis), shard.shape[dim])
    up = [(i, (i + 1) % size) for i in range(size - 1)]
    down = [(j, i) for i, j in up]
    last = lax.slice_in_dim(shard, length - width, length, axis=dim)
    leading = lax.slice_in_dim(shard, 0, width, axis=dim)
    return (lax.ppermute(last, axis, up), lax.ppermute(leading, axis, down))


VMEM = pl.BlockSpec(memory_space=pltpu.VMEM)
SMEM = pl.BlockSpec(memory_space=pltpu.SMEM)


def scratch(slab_z, rows_y, width):
    rows = ZC * rows_y
    deep = rows_y + 2 * HALO
    return [
        pltpu.VMEM((slab_z + 2 * HALO, deep, width), F32),
        pltpu.VMEM((6 * ZC, deep, width), BF16),
        pltpu.VMEM((6 * ZC, deep, width), BF16),
        pltpu.VMEM((12, rows, width), F32),
        pltpu.VMEM((16 * rows, width), F32),
        pltpu.VMEM((16 * rows, width), F32),
        pltpu.VMEM((4 * rows, width), F32),
        pltpu.VMEM((4 * rows, width), F32),
    ]


def cost(share):
    return pl.CostEstimate(
        flops=int(share * 28e9), bytes_accessed=int(share * 4e6), transcendentals=int(share * 4e5)
    )


PARAMS = pltpu.CompilerParams(vmem_limit_bytes=58 * 1024 * 1024)


def inner_sums(own, labels, matrices):
    return pl.pallas_call(
        inner_kernel,
        out_shape=(
            jax.ShapeDtypeStruct(labels.shape, BF16),
            jax.ShapeDtypeStruct((HI * FEAT, LO), F32),
        ),
        in_specs=[VMEM] * 5,
        out_specs=(VMEM, VMEM),
        scratch_shapes=scratch(*labels.shape),
        compiler_params=PARAMS,
        cost_estimate=cost(0.25),
    )(own, labels, *matrices)


def outer_sums(owners, ranks, before, own, after, labels, matrices, inner, groups, quarters):
    return pl.pallas_call(
        outer_kernel,
        out_shape=(
            jax.ShapeDtypeStruct(labels.shape, BF16),
            jax.ShapeDtypeStruct((groups, quarters, SEND, LBL), BF16),
        ),
        in_specs=[SMEM] * 2 + [VMEM] * 9,
        out_specs=(VMEM, VMEM),
        scratch_shapes=scratch(*labels.shape)
        + [pltpu.VMEM((HI * FEAT, LO), F32), pltpu.VMEM((FEAT, LBL), F32)],
        compiler_params=PARAMS,
        cost_estimate=cost(0.75),
    )(owners, ranks, before, own, after, labels, *matrices, *inner)


def local(image, labels, brick_blocks, block_owner):
    groups = lax.axis_size("gy")
    quarters = lax.axis_size("gz")
    listed_count = brick_blocks.shape[-1]
    total_blocks = block_owner.shape[0]
    blk_dev = total_blocks // groups
    block_index = jnp.arange(total_blocks, dtype=jnp.int32)
    earlier = (block_index[None, :] < block_index[:, None]) & (
        block_owner[None, :] == block_owner[:, None]
    )
    owner_rank = jnp.sum(earlier.astype(jnp.int32), axis=1)
    listed_ids = brick_blocks.reshape(listed_count)
    listed = (listed_ids[:, None] == block_index[None, :]).astype(jnp.int32)
    owners = jnp.sum(listed * block_owner[None, :], axis=1)
    ranks = jnp.sum(listed * owner_rank[None, :], axis=1)

    matrices = filter_matrices(*labels.shape[1:])
    left, right = extended(image, "gy", 1, HALO)
    own = jnp.concatenate([left, image, right], axis=1)
    before, after = extended(own, "gz", 0, HALO)
    inner = inner_sums(own, labels, matrices)
    likeness, message = outer_sums(
        owners, ranks, before, own, after, labels, matrices, inner, groups, quarters
    )
    message = message.reshape(groups * quarters, SEND, LBL)
    got = lax.all_to_all(message, ("gy", "gz"), 0, 0, tiled=True)
    label_features = pl.pallas_call(
        sum_kernel,
        out_shape=jax.ShapeDtypeStruct((blk_dev, FEAT // quarters, LBL), F32),
    )(got)
    return (likeness, label_features)


def solution(mesh):
    placed = (P("gz", "gy", None), P("gz", "gy", None), P("gz", "gy", None), P())
    return jax.shard_map(
        local,
        mesh=mesh,
        in_specs=placed,
        out_specs=(P("gz", "gy", None), P("gy", "gz", None)),
        check_vma=False,
    )
```

```python
import math

import jax
import jax.numpy as jnp
import ml_dtypes
import numpy as np
from jax import lax
from jax.experimental import pallas as pl
from jax.experimental.pallas import tpu as pltpu
from jax.sharding import PartitionSpec as P

LBL = 128
FEAT = 64
HALO = 12
ZC_IN, ZC_OUT = (8, 6)
PLANES_IN, PLANES_OUT = (4, 3)
SIGMAS = (2, 4)
CENTERS = (-1.5, -0.5, 0.5, 1.5)
ORDERS = ((2, 0, 0), (0, 2, 0), (0, 0, 2), (1, 1, 0), (1, 0, 1), (0, 1, 1))
HI = 8
LO = 256
SEND = 24
F32, BF16 = jnp.float32, jnp.bfloat16


def kernel_set(sigma_val):
    radius = 3 * sigma_val
    offsets = [float(step) for step in range(-radius, radius + 1)]
    smooth = [math.exp(-step * step / (2.0 * sigma_val**2)) for step in offsets]
    weight_total = sum(smooth)
    smooth = [value / weight_total for value in smooth]
    first_order = [step / sigma_val**2 * value for step, value in zip(offsets, smooth)]
    second = [
        (step * step / sigma_val**4 - 1.0 / sigma_val**2) * value
        for step, value in zip(offsets, smooth)
    ]
    return (radius, [smooth, first_order, second])


def banded(weights, radius, rows, columns, offset):
    matrix = np.zeros((rows, columns))
    for row in range(rows):
        for tap, weight in enumerate(weights):
            column = row + offset + tap - radius
            if 0 <= column < columns:
                matrix[row, column] = weight
    return matrix


def two_parts(matrix):
    high = matrix.astype(np.float32).astype(ml_dtypes.bfloat16)
    low = (matrix - high.astype(np.float64)).astype(np.float32).astype(ml_dtypes.bfloat16)
    return (high, low)


def filter_matrices(chunk, rows_y, width):
    along_z, along_y, along_x = ([], [], [])
    for sigma_val in SIGMAS:
        radius, filters = kernel_set(sigma_val)
        y_rows = []
        for order in range(3):
            z_matrix = banded(filters[order], radius, chunk, chunk + 2 * HALO, HALO)
            along_z.append(np.kron(z_matrix, np.eye(8)))
            y_rows.append(banded(filters[order], radius, rows_y, rows_y + 2 * HALO, HALO))
            x_matrix = banded(filters[order], radius, width, width, 0).T
            parts = np.concatenate(two_parts(x_matrix * (4.0 * sigma_val**3.5)), axis=1)
            along_x.append(np.concatenate([parts, parts], axis=0))
        y_matrix = np.concatenate(y_rows)
        y_matrix = np.pad(y_matrix, ((0, -y_matrix.shape[0] % 16), (0, 0)))
        high, low = two_parts(y_matrix)
        along_y.append(np.concatenate([high, high, low], axis=1))
    z_parts = np.concatenate(two_parts(np.concatenate(along_z)), axis=0)
    return (z_parts, np.stack(along_y), np.stack(along_x))


def split(value):
    high = value.astype(BF16)
    return (high, (value - high.astype(F32)).astype(BF16))


def filters_of(
    z_start, chunk, ext, wz_ref, wy_ref, wx_ref, z_high, z_low, y_out, channels, bands, like_ref
):
    rows_y, width = like_ref.shape[1:]
    deep = rows_y + 2 * HALO
    rows = chunk * rows_y
    planes = 6 * chunk

    for pair in range(deep // 16):
        tiles = [
            ext[pl.ds(z_start, chunk + 2 * HALO), pl.ds(16 * pair + 8 * half, 8), :]
            .reshape((chunk + 2 * HALO) * 8, width)
            .astype(BF16)
            for half in range(2)
        ]
        out = jnp.dot(wz_ref[...], jnp.concatenate(tiles, axis=1), preferred_element_type=F32)
        out = (out[: planes * 8] + out[planes * 8 :]).reshape(planes, 8, 2 * width)
        out = jnp.concatenate([out[:, :, :width], out[:, :, width:]], axis=1)
        high, low = split(out)
        z_high[:, pl.ds(16 * pair, 16), :] = high
        z_low[:, pl.ds(16 * pair, 16), :] = low

    for scale in range(2):
        for order_z in range(3):
            for pair in range(chunk // 2):
                columns = []
                for half in range(2):
                    index = (scale * 3 + order_z) * chunk + 2 * pair + half
                    columns.append(
                        jnp.concatenate([z_high[index], z_low[index], z_high[index]], axis=0)
                    )
                deep_rows = jnp.concatenate(columns, axis=1)
                count = wy_ref.shape[1] if order_z == 0 else (48 if order_z == 1 else 32)
                out = jnp.dot(
                    wy_ref[scale, :count, :], deep_rows, preferred_element_type=F32
                )
                for order_y in range(3 - order_z):
                    component = [
                        i for i, o in enumerate(ORDERS) if o[1:] == (order_y, order_z)
                    ][0]
                    for half in range(2):
                        y_out[
                            scale * 6 + component, pl.ds((2 * pair + half) * rows_y, rows_y), :
                        ] = out[
                            order_y * rows_y : (order_y + 1) * rows_y,
                            half * width : (half + 1) * width,
                        ]

    tubes = []
    for scale in range(2):
        hessian = [None] * 6
        for order_x in range(3):
            members = [i for i, o in enumerate(ORDERS) if o[0] == order_x]
            two = [jnp.concatenate(split(y_out[scale * 6 + i]), axis=1) for i in members]
            out = jnp.dot(
                jnp.concatenate(two, axis=0),
                wx_ref[scale * 3 + order_x],
                preferred_element_type=F32,
            )
            out = out[:, :width] + out[:, width:]
            for index, member in enumerate(members):
                hessian[member] = out[index * rows : (index + 1) * rows]
        xx, yy, zz, xy, xz, yz = hessian
        trace = xx + yy + zz
        frob = xx * xx + yy * yy + zz * zz + 2.0 * (xy * xy + xz * xz + yz * yz)
        minors = 0.5 * (trace * trace - frob)
        tube = jnp.maximum(-trace, 0.0) * jnp.maximum(minors, 0.0) / (frob + 0.25)
        tubes.append(tube)
        for index, value in enumerate(hessian + [minors, tube]):
            channels[pl.ds((scale * 8 + index) * rows, rows), :] = value
    like = jnp.maximum(tubes[0], tubes[1])
    like_ref[pl.ds(z_start, chunk)] = like.reshape(chunk, rows_y, width).astype(BF16)

    volume = ext[pl.ds(z_start + HALO, chunk), pl.ds(HALO, rows_y), :].reshape(rows, width)
    for index, center in enumerate(CENTERS):
        bands[pl.ds(index * rows, rows), :] = jnp.exp(-((volume - center) ** 2))


def add_sums(z_start, chunk, planes, labels_ref, channels, bands, acc):
    rows_y, width = labels_ref.shape[1:]
    rows = chunk * rows_y
    group = planes * rows_y
    low_ids = lax.broadcasted_iota(jnp.int32, (LO, width), 0).astype(F32).astype(BF16)

    def step(part, carry):
        left, right = ([], [])
        marks = labels_ref[pl.ds(z_start + part * planes, planes)].reshape(group, width)
        mark_high = (marks >> 8).astype(F32)
        mark_low = (marks & 255).astype(F32)
        for row in range(group):
            at = part * group + row
            feats = []
            for scale in range(2):
                base = channels[pl.ds(scale * 8 * rows + at, 8, stride=rows), :]
                for band in range(4):
                    feats.append(base * bands[pl.ds(band * rows + at, 1), :])
            feats = jnp.concatenate(feats, axis=0).astype(BF16)
            high_of = jnp.broadcast_to(mark_high[row : row + 1], (FEAT, width)).astype(BF16)
            low_of = jnp.broadcast_to(mark_low[row : row + 1], (LO, width)).astype(BF16)
            zero = jnp.zeros_like(feats)
            left.append(
                jnp.concatenate(
                    [jnp.where(high_of == jnp.asarray(h, BF16), feats, zero) for h in range(HI)],
                    axis=0,
                )
            )
            right.append(
                jnp.where(low_of == low_ids, jnp.asarray(1, BF16), jnp.asarray(0, BF16))
            )
        acc[...] += lax.dot_general(
            jnp.concatenate(left, axis=1),
            jnp.concatenate(right, axis=1),
            (((1,), (1,)), ((), ())),
            preferred_element_type=F32,
        )
        return carry

    lax.fori_loop(0, chunk // planes, step, 0)


def all_chunks(start_of, count, chunk, planes, ext, labels_ref, weights, passes, buffers, acc, like_ref):
    def step(index, carry):
        z_start = start_of(index)
        filters_of(z_start, chunk, ext, *weights, *passes, *buffers, like_ref)
        add_sums(z_start, chunk, planes, labels_ref, *buffers, acc)
        return carry

    lax.fori_loop(0, count, step, 0)


def inner_kernel(
    own_ref, labels_ref, wz_ref, wy_ref, wx_ref,
    like_ref, acc,
    ext, z_high, z_low, y_out, channels, bands,
):
    slab_z = labels_ref.shape[0]
    ext[pl.ds(HALO, slab_z)] = own_ref[...].astype(F32)
    acc[...] = jnp.zeros_like(acc)
    all_chunks(
        lambda index: HALO + index * ZC_IN, (slab_z - 2 * HALO) // ZC_IN, ZC_IN, PLANES_IN, ext, labels_ref,
        (wz_ref, wy_ref, wx_ref), (z_high, z_low, y_out),
        (channels, bands), acc, like_ref,
    )


def outer_kernel(
    owner_ref, rank_ref, ends_ref, before_ref, own_ref, after_ref, labels_ref, wz_ref, wy_ref,
    wx_ref, inner_like_ref, inner_acc_ref,
    like_ref, send_ref,
    ext, z_high, z_low, y_out, channels, bands, acc, turned,
):
    slab_z = labels_ref.shape[0]
    ext[pl.ds(HALO, slab_z)] = own_ref[...].astype(F32)
    for end, (ref, at) in enumerate(((before_ref, 0), (after_ref, HALO + slab_z))):
        ext[pl.ds(at, HALO)] = jnp.where(ends_ref[end] != 0, 0.0, ref[...].astype(F32))
    acc[...] = inner_acc_ref[...]
    inner = pl.ds(HALO, slab_z - 2 * HALO)
    like_ref[inner] = inner_like_ref[inner]
    half = HALO // ZC_OUT

    def start_of(index):
        return index * ZC_OUT + jnp.where(index >= half, slab_z - 2 * HALO, 0)

    all_chunks(
        start_of, 2 * half, ZC_OUT, PLANES_OUT, ext, labels_ref,
        (wz_ref, wy_ref, wx_ref), (z_high, z_low, y_out),
        (channels, bands), acc, like_ref,
    )

    send_ref[...] = jnp.zeros_like(send_ref)
    for slot in range(owner_ref.shape[0]):
        owner = owner_ref[slot]
        rank = rank_ref[slot].astype(F32)
        for scale in range(2):
            for band in range(4):
                turned[pl.ds(32 * scale + band, 8, stride=4), :] = acc[
                    pl.ds((slot // 2) * FEAT + 32 * scale + 8 * band, 8),
                    pl.ds((slot % 2) * LBL, LBL),
                ]
        for quarter in range(4):
            send_ref[owner, quarter, pl.ds(0, 16), :] = turned[pl.ds(16 * quarter, 16), :].astype(
                BF16
            )
            send_ref[owner, quarter, pl.ds(16, 8), :] = jnp.full((8, LBL), rank, F32).astype(BF16)


def sum_kernel(got_ref, out_ref):
    sources = got_ref.shape[0]

    def step(source, totals):
        block = got_ref[source].astype(F32)
        data, rank = (block[:16], jnp.concatenate([block[16:], block[16:]], axis=0))
        return tuple(
            total + jnp.where(rank == float(index), data, 0.0) for index, total in enumerate(totals)
        )

    totals = lax.fori_loop(
        0,
        sources,
        step,
        tuple(jnp.zeros(out_ref.shape[1:], F32) for _ in range(out_ref.shape[0])),
        unroll=8,
    )
    for index, total in enumerate(totals):
        out_ref[index] = total


def neighbours(shard, axis, dim, width):
    size, length = (lax.axis_size(axis), shard.shape[dim])
    up = [(i, (i + 1) % size) for i in range(size)]
    down = [(j, i) for i, j in up]
    last = lax.slice_in_dim(shard, length - width, length, axis=dim)
    leading = lax.slice_in_dim(shard, 0, width, axis=dim)
    here = lax.axis_index(axis)
    ends = (here == 0, here == size - 1)
    return (lax.ppermute(last, axis, up), lax.ppermute(leading, axis, down), ends)


VMEM = pl.BlockSpec(memory_space=pltpu.VMEM)
SMEM = pl.BlockSpec(memory_space=pltpu.SMEM)


def scratch(chunk, slab_z, rows_y, width):
    rows = chunk * rows_y
    deep = rows_y + 2 * HALO
    return [
        pltpu.VMEM((slab_z + 2 * HALO, deep, width), F32),
        pltpu.VMEM((6 * chunk, deep, width), BF16),
        pltpu.VMEM((6 * chunk, deep, width), BF16),
        pltpu.VMEM((12, rows, width), F32),
        pltpu.VMEM((16 * rows, width), F32),
        pltpu.VMEM((4 * rows, width), F32),
    ]


def cost(share):
    return pl.CostEstimate(
        flops=int(share * 28e9), bytes_accessed=int(share * 4e6), transcendentals=int(share * 4e5)
    )


PARAMS = pltpu.CompilerParams(vmem_limit_bytes=36 * 1024 * 1024)


def inner_sums(own, labels):
    matrices = filter_matrices(ZC_IN, *labels.shape[1:])
    return pl.pallas_call(
        inner_kernel,
        out_shape=(
            jax.ShapeDtypeStruct(labels.shape, BF16),
            jax.ShapeDtypeStruct((HI * FEAT, LO), F32),
        ),
        in_specs=[VMEM] * 5,
        out_specs=(VMEM, VMEM),
        scratch_shapes=scratch(ZC_IN, *labels.shape),
        compiler_params=PARAMS,
        cost_estimate=cost(0.25),
    )(own, labels, *matrices)


def outer_sums(owners, ranks, ends, before, own, after, labels, inner, groups, quarters):
    matrices = filter_matrices(ZC_OUT, *labels.shape[1:])
    return pl.pallas_call(
        outer_kernel,
        out_shape=(
            jax.ShapeDtypeStruct(labels.shape, BF16),
            jax.ShapeDtypeStruct((groups, quarters, SEND, LBL), BF16),
        ),
        in_specs=[SMEM] * 3 + [VMEM] * 9,
        out_specs=(VMEM, VMEM),
        scratch_shapes=scratch(ZC_OUT, *labels.shape)
        + [pltpu.VMEM((HI * FEAT, LO), F32), pltpu.VMEM((FEAT, LBL), F32)],
        compiler_params=PARAMS,
        cost_estimate=cost(0.75),
    )(owners, ranks, ends, before, own, after, labels, *matrices, *inner)


def local(image, labels, brick_blocks, block_owner):
    groups = lax.axis_size("gy")
    quarters = lax.axis_size("gz")
    listed_count = brick_blocks.shape[-1]
    total_blocks = block_owner.shape[0]
    blk_dev = total_blocks // groups
    block_index = jnp.arange(total_blocks, dtype=jnp.int32)
    earlier = (block_index[None, :] < block_index[:, None]) & (
        block_owner[None, :] == block_owner[:, None]
    )
    owner_rank = jnp.sum(earlier.astype(jnp.int32), axis=1)
    listed_ids = brick_blocks.reshape(listed_count)
    listed = (listed_ids[:, None] == block_index[None, :]).astype(jnp.int32)
    owners = jnp.sum(listed * block_owner[None, :], axis=1)
    ranks = jnp.sum(listed * owner_rank[None, :], axis=1)

    left, right, (first, last) = neighbours(image, "gy", 1, HALO)
    zero = jnp.zeros((), image.dtype)
    own = jnp.concatenate(
        [jnp.where(first, zero, left), image, jnp.where(last, zero, right)], axis=1
    )
    before, after, ends = neighbours(own, "gz", 0, HALO)
    inner = inner_sums(own, labels)
    likeness, message = outer_sums(
        owners, ranks, jnp.stack(ends).astype(jnp.int32), before, own, after, labels, inner,
        groups, quarters,
    )
    message = message.reshape(groups * quarters, SEND, LBL)
    got = lax.all_to_all(message, ("gy", "gz"), 0, 0, tiled=True)
    label_features = pl.pallas_call(
        sum_kernel,
        out_shape=jax.ShapeDtypeStruct((blk_dev, FEAT // quarters, LBL), F32),
    )(got)
    return (likeness, label_features)


def solution(mesh):
    placed = (P("gz", "gy", None), P("gz", "gy", None), P("gz", "gy", None), P())
    return jax.shard_map(
        local,
        mesh=mesh,
        in_specs=placed,
        out_specs=(P("gz", "gy", None), P("gy", "gz", None)),
        check_vma=False,
    )
```

```python
import math

import jax
import jax.numpy as jnp
import ml_dtypes
import numpy as np
from jax import lax
from jax.experimental import pallas as pl
from jax.experimental.pallas import tpu as pltpu
from jax.sharding import PartitionSpec as P

LBL = 128
FEAT = 64
HALO = 12
ZC_IN, ZC_OUT = (8, 12)
ZP_IN, ZP_OUT = (8, 6)
PLANES_IN, PLANES_OUT = (4, 4)
SIGMAS = (2, 4)
CENTERS = (-1.5, -0.5, 0.5, 1.5)
ORDERS = ((2, 0, 0), (0, 2, 0), (0, 0, 2), (1, 1, 0), (1, 0, 1), (0, 1, 1))
HI = 8
LO = 256
SEND = 24
F32, BF16 = jnp.float32, jnp.bfloat16


def kernel_set(sigma_val):
    radius = 3 * sigma_val
    offsets = [float(step) for step in range(-radius, radius + 1)]
    smooth = [math.exp(-step * step / (2.0 * sigma_val**2)) for step in offsets]
    weight_total = sum(smooth)
    smooth = [value / weight_total for value in smooth]
    first_order = [step / sigma_val**2 * value for step, value in zip(offsets, smooth)]
    second = [
        (step * step / sigma_val**4 - 1.0 / sigma_val**2) * value
        for step, value in zip(offsets, smooth)
    ]
    return (radius, [smooth, first_order, second])


def banded(weights, radius, rows, columns, offset):
    matrix = np.zeros((rows, columns))
    for row in range(rows):
        for tap, weight in enumerate(weights):
            column = row + offset + tap - radius
            if 0 <= column < columns:
                matrix[row, column] = weight
    return matrix


def two_parts(matrix):
    high = matrix.astype(np.float32).astype(ml_dtypes.bfloat16)
    low = (matrix - high.astype(np.float64)).astype(np.float32).astype(ml_dtypes.bfloat16)
    return (high, low)


def filter_matrices(chunk, rows_y, width):
    along_z, along_y, along_x = ([], [], [])
    for sigma_val in SIGMAS:
        radius, filters = kernel_set(sigma_val)
        y_rows = []
        for order in range(3):
            z_matrix = banded(filters[order], radius, chunk, chunk + 2 * HALO, HALO)
            along_z.append(np.kron(z_matrix, np.eye(8)))
            y_rows.append(banded(filters[order], radius, rows_y, rows_y + 2 * HALO, HALO))
            x_matrix = banded(filters[order], radius, width, width, 0).T
            parts = np.concatenate(two_parts(x_matrix * (4.0 * sigma_val**3.5)), axis=1)
            along_x.append(np.concatenate([parts, parts], axis=0))
        y_matrix = np.concatenate(y_rows)
        y_matrix = np.pad(y_matrix, ((0, -y_matrix.shape[0] % 16), (0, 0)))
        high, low = two_parts(y_matrix)
        along_y.append(np.concatenate([high, high, low], axis=1))
    z_parts = np.concatenate(two_parts(np.concatenate(along_z)), axis=0)
    return (z_parts, np.stack(along_y), np.stack(along_x))


def split(value):
    high = value.astype(BF16)
    return (high, (value - high.astype(F32)).astype(BF16))


def filters_of(
    z_start, chunk, ext, wz_ref, wy_ref, wx_ref, z_high, z_low, y_out, channels, bands, like_ref
):
    rows_y, width = like_ref.shape[1:]
    deep = rows_y + 2 * HALO
    rows = chunk * rows_y
    piece = wz_ref.shape[0] // (2 * 6 * 8)
    planes = 6 * piece

    for first in range(0, chunk, piece):
        for pair in range(deep // 16):
            tiles = [
                ext[pl.ds(z_start + first, piece + 2 * HALO), pl.ds(16 * pair + 8 * half, 8), :]
                .reshape((piece + 2 * HALO) * 8, width)
                .astype(BF16)
                for half in range(2)
            ]
            out = jnp.dot(wz_ref[...], jnp.concatenate(tiles, axis=1), preferred_element_type=F32)
            out = (out[: planes * 8] + out[planes * 8 :]).reshape(planes, 8, 2 * width)
            out = jnp.concatenate([out[:, :, :width], out[:, :, width:]], axis=1)
            high, low = split(out.reshape(6, piece, 16, width))
            z_high[:, pl.ds(first, piece), pl.ds(16 * pair, 16), :] = high
            z_low[:, pl.ds(first, piece), pl.ds(16 * pair, 16), :] = low

    for scale in range(2):
        for order_z in range(3):
            for pair in range(chunk // 2):
                columns = []
                for half in range(2):
                    index = (scale * 3 + order_z, 2 * pair + half)
                    columns.append(
                        jnp.concatenate([z_high[index], z_low[index], z_high[index]], axis=0)
                    )
                deep_rows = jnp.concatenate(columns, axis=1)
                count = (3 - order_z) * rows_y
                out = jnp.dot(
                    wy_ref[scale, :count, :], deep_rows, preferred_element_type=F32
                )
                for order_y in range(3 - order_z):
                    component = [
                        i for i, o in enumerate(ORDERS) if o[1:] == (order_y, order_z)
                    ][0]
                    for half in range(2):
                        y_out[
                            scale * 6 + component, pl.ds((2 * pair + half) * rows_y, rows_y), :
                        ] = out[
                            order_y * rows_y : (order_y + 1) * rows_y,
                            half * width : (half + 1) * width,
                        ]

    tubes = []
    for scale in range(2):
        hessian = [None] * 6
        for order_x in range(3):
            members = [i for i, o in enumerate(ORDERS) if o[0] == order_x]
            two = [jnp.concatenate(split(y_out[scale * 6 + i]), axis=1) for i in members]
            out = jnp.dot(
                jnp.concatenate(two, axis=0),
                wx_ref[scale * 3 + order_x],
                preferred_element_type=F32,
            )
            out = out[:, :width] + out[:, width:]
            for index, member in enumerate(members):
                hessian[member] = out[index * rows : (index + 1) * rows]
        xx, yy, zz, xy, xz, yz = hessian
        trace = xx + yy + zz
        frob = xx * xx + yy * yy + zz * zz + 2.0 * (xy * xy + xz * xz + yz * yz)
        minors = 0.5 * (trace * trace - frob)
        tube = jnp.maximum(-trace, 0.0) * jnp.maximum(minors, 0.0) / (frob + 0.25)
        tubes.append(tube)
        for index, value in enumerate(hessian + [minors, tube]):
            channels[pl.ds((scale * 8 + index) * rows, rows), :] = value
    like = jnp.maximum(tubes[0], tubes[1])
    like_ref[pl.ds(z_start, chunk)] = like.reshape(chunk, rows_y, width).astype(BF16)

    volume = ext[pl.ds(z_start + HALO, chunk), pl.ds(HALO, rows_y), :].reshape(rows, width)
    for index, center in enumerate(CENTERS):
        bands[pl.ds(index * rows, rows), :] = jnp.exp(-((volume - center) ** 2))


def add_sums(z_start, chunk, planes, labels_ref, channels, bands, acc):
    rows_y, width = labels_ref.shape[1:]
    rows = chunk * rows_y
    group = planes * rows_y
    low_ids = lax.broadcasted_iota(jnp.int32, (LO, width), 0).astype(F32).astype(BF16)

    def step(part, carry):
        left, right = ([], [])
        marks = labels_ref[pl.ds(z_start + part * planes, planes)].reshape(group, width)
        mark_high = (marks >> 8).astype(F32)
        mark_low = (marks & 255).astype(F32)
        for row in range(group):
            at = part * group + row
            feats = []
            for scale in range(2):
                base = channels[pl.ds(scale * 8 * rows + at, 8, stride=rows), :]
                for band in range(4):
                    feats.append(base * bands[pl.ds(band * rows + at, 1), :])
            feats = jnp.concatenate(feats, axis=0).astype(BF16)
            high_of = jnp.broadcast_to(mark_high[row : row + 1], (FEAT, width)).astype(BF16)
            low_of = jnp.broadcast_to(mark_low[row : row + 1], (LO, width)).astype(BF16)
            zero = jnp.zeros_like(feats)
            left.append(
                jnp.concatenate(
                    [jnp.where(high_of == jnp.asarray(h, BF16), feats, zero) for h in range(HI)],
                    axis=0,
                )
            )
            right.append(
                jnp.where(low_of == low_ids, jnp.asarray(1, BF16), jnp.asarray(0, BF16))
            )
        acc[...] += lax.dot_general(
            jnp.concatenate(left, axis=1),
            jnp.concatenate(right, axis=1),
            (((1,), (1,)), ((), ())),
            preferred_element_type=F32,
        )
        return carry

    lax.fori_loop(0, chunk // planes, step, 0)


def all_chunks(start_of, count, chunk, planes, ext, labels_ref, weights, passes, buffers, acc, like_ref):
    def step(index, carry):
        z_start = start_of(index)
        filters_of(z_start, chunk, ext, *weights, *passes, *buffers, like_ref)
        add_sums(z_start, chunk, planes, labels_ref, *buffers, acc)
        return carry

    lax.fori_loop(0, count, step, 0)


def inner_kernel(
    own_ref, labels_ref, wz_ref, wy_ref, wx_ref,
    like_ref, acc,
    ext, z_high, z_low, y_out, channels, bands,
):
    slab_z = labels_ref.shape[0]
    ext[pl.ds(HALO, slab_z)] = own_ref[...].astype(F32)
    acc[...] = jnp.zeros_like(acc)
    all_chunks(
        lambda index: HALO + index * ZC_IN, (slab_z - 2 * HALO) // ZC_IN, ZC_IN, PLANES_IN, ext, labels_ref,
        (wz_ref, wy_ref, wx_ref), (z_high, z_low, y_out),
        (channels, bands), acc, like_ref,
    )


def outer_kernel(
    owner_ref, rank_ref, ends_ref, before_ref, own_ref, after_ref, labels_ref, wz_ref, wy_ref,
    wx_ref, inner_like_ref, inner_acc_ref,
    like_ref, send_ref,
    ext, z_high, z_low, y_out, channels, bands, acc, turned,
):
    slab_z = labels_ref.shape[0]
    ext[pl.ds(HALO, slab_z)] = own_ref[...].astype(F32)
    for end, (ref, at) in enumerate(((before_ref, 0), (after_ref, HALO + slab_z))):
        ext[pl.ds(at, HALO)] = jnp.where(ends_ref[end] != 0, 0.0, ref[...].astype(F32))
    acc[...] = inner_acc_ref[...]
    inner = pl.ds(HALO, slab_z - 2 * HALO)
    like_ref[inner] = inner_like_ref[inner]
    half = HALO // ZC_OUT

    def start_of(index):
        return index * ZC_OUT + jnp.where(index >= half, slab_z - 2 * HALO, 0)

    all_chunks(
        start_of, 2 * half, ZC_OUT, PLANES_OUT, ext, labels_ref,
        (wz_ref, wy_ref, wx_ref), (z_high, z_low, y_out),
        (channels, bands), acc, like_ref,
    )

    send_ref[...] = jnp.zeros_like(send_ref)
    for slot in range(owner_ref.shape[0]):
        owner = owner_ref[slot]
        rank = rank_ref[slot].astype(F32)
        for scale in range(2):
            for band in range(4):
                turned[pl.ds(32 * scale + band, 8, stride=4), :] = acc[
                    pl.ds((slot // 2) * FEAT + 32 * scale + 8 * band, 8),
                    pl.ds((slot % 2) * LBL, LBL),
                ]
        for quarter in range(4):
            send_ref[owner, quarter, pl.ds(0, 16), :] = turned[pl.ds(16 * quarter, 16), :].astype(
                BF16
            )
            send_ref[owner, quarter, pl.ds(16, 8), :] = jnp.full((8, LBL), rank, F32).astype(BF16)


def sum_kernel(got_ref, out_ref):
    sources = got_ref.shape[0]

    def step(source, totals):
        block = got_ref[source].astype(F32)
        data, rank = (block[:16], jnp.concatenate([block[16:], block[16:]], axis=0))
        return tuple(
            total + jnp.where(rank == float(index), data, 0.0) for index, total in enumerate(totals)
        )

    totals = lax.fori_loop(
        0,
        sources,
        step,
        tuple(jnp.zeros(out_ref.shape[1:], F32) for _ in range(out_ref.shape[0])),
        unroll=8,
    )
    for index, total in enumerate(totals):
        out_ref[index] = total


def neighbours(shard, axis, dim, width):
    size, length = (lax.axis_size(axis), shard.shape[dim])
    up = [(i, (i + 1) % size) for i in range(size)]
    down = [(j, i) for i, j in up]
    last = lax.slice_in_dim(shard, length - width, length, axis=dim)
    leading = lax.slice_in_dim(shard, 0, width, axis=dim)
    here = lax.axis_index(axis)
    ends = (here == 0, here == size - 1)
    return (lax.ppermute(last, axis, up), lax.ppermute(leading, axis, down), ends)


VMEM = pl.BlockSpec(memory_space=pltpu.VMEM)
SMEM = pl.BlockSpec(memory_space=pltpu.SMEM)


def scratch(chunk, slab_z, rows_y, width):
    rows = chunk * rows_y
    deep = rows_y + 2 * HALO
    return [
        pltpu.VMEM((slab_z + 2 * HALO, deep, width), F32),
        pltpu.VMEM((6, chunk, deep, width), BF16),
        pltpu.VMEM((6, chunk, deep, width), BF16),
        pltpu.VMEM((12, rows, width), F32),
        pltpu.VMEM((16 * rows, width), F32),
        pltpu.VMEM((4 * rows, width), F32),
    ]


def cost(share):
    return pl.CostEstimate(
        flops=int(share * 28e9), bytes_accessed=int(share * 4e6), transcendentals=int(share * 4e5)
    )


PARAMS = pltpu.CompilerParams(vmem_limit_bytes=36 * 1024 * 1024)


def inner_sums(own, labels):
    matrices = filter_matrices(ZP_IN, *labels.shape[1:])
    return pl.pallas_call(
        inner_kernel,
        out_shape=(
            jax.ShapeDtypeStruct(labels.shape, BF16),
            jax.ShapeDtypeStruct((HI * FEAT, LO), F32),
        ),
        in_specs=[VMEM] * 5,
        out_specs=(VMEM, VMEM),
        scratch_shapes=scratch(ZC_IN, *labels.shape),
        compiler_params=PARAMS,
        cost_estimate=cost(0.25),
    )(own, labels, *matrices)


def outer_sums(owners, ranks, ends, before, own, after, labels, inner, groups, quarters):
    matrices = filter_matrices(ZP_OUT, *labels.shape[1:])
    return pl.pallas_call(
        outer_kernel,
        out_shape=(
            jax.ShapeDtypeStruct(labels.shape, BF16),
            jax.ShapeDtypeStruct((groups, quarters, SEND, LBL), BF16),
        ),
        in_specs=[SMEM] * 3 + [VMEM] * 9,
        out_specs=(VMEM, VMEM),
        scratch_shapes=scratch(ZC_OUT, *labels.shape)
        + [pltpu.VMEM((HI * FEAT, LO), F32), pltpu.VMEM((FEAT, LBL), F32)],
        compiler_params=PARAMS,
        cost_estimate=cost(0.75),
    )(owners, ranks, ends, before, own, after, labels, *matrices, *inner)


def local(image, labels, brick_blocks, block_owner):
    groups = lax.axis_size("gy")
    quarters = lax.axis_size("gz")
    listed_count = brick_blocks.shape[-1]
    total_blocks = block_owner.shape[0]
    blk_dev = total_blocks // groups
    block_index = jnp.arange(total_blocks, dtype=jnp.int32)
    earlier = (block_index[None, :] < block_index[:, None]) & (
        block_owner[None, :] == block_owner[:, None]
    )
    owner_rank = jnp.sum(earlier.astype(jnp.int32), axis=1)
    listed_ids = brick_blocks.reshape(listed_count)
    listed = (listed_ids[:, None] == block_index[None, :]).astype(jnp.int32)
    owners = jnp.sum(listed * block_owner[None, :], axis=1)
    ranks = jnp.sum(listed * owner_rank[None, :], axis=1)

    left, right, (first, last) = neighbours(image, "gy", 1, HALO)
    zero = jnp.zeros((), image.dtype)
    own = jnp.concatenate(
        [jnp.where(first, zero, left), image, jnp.where(last, zero, right)], axis=1
    )
    before, after, ends = neighbours(own, "gz", 0, HALO)
    inner = inner_sums(own, labels)
    likeness, message = outer_sums(
        owners, ranks, jnp.stack(ends).astype(jnp.int32), before, own, after, labels, inner,
        groups, quarters,
    )
    message = message.reshape(groups * quarters, SEND, LBL)
    got = lax.all_to_all(message, ("gy", "gz"), 0, 0, tiled=True)
    label_features = pl.pallas_call(
        sum_kernel,
        out_shape=jax.ShapeDtypeStruct((blk_dev, FEAT // quarters, LBL), F32),
        compiler_params=pltpu.CompilerParams(vmem_limit_bytes=6 * 1024 * 1024),
    )(got)
    return (likeness, label_features)


def solution(mesh):
    placed = (P("gz", "gy", None), P("gz", "gy", None), P("gz", "gy", None), P())
    return jax.shard_map(
        local,
        mesh=mesh,
        in_specs=placed,
        out_specs=(P("gz", "gy", None), P("gy", "gz", None)),
        check_vma=False,
    )
```

```python
import math

import jax
import jax.numpy as jnp
import ml_dtypes
import numpy as np
from jax import lax
from jax.experimental import pallas as pl
from jax.experimental.pallas import tpu as pltpu
from jax.sharding import PartitionSpec as P

LBL = 128
FEAT = 64
HALO = 12
ZC_IN, ZC_OUT = (8, 12)
ZP_IN, ZP_OUT = (8, 6)
PLANES_IN, PLANES_OUT = (4, 6)
SIGMAS = (2, 4)
CENTERS = (-1.5, -0.5, 0.5, 1.5)
ORDERS = ((2, 0, 0), (0, 2, 0), (0, 0, 2), (1, 1, 0), (1, 0, 1), (0, 1, 1))
HI = 8
LO = 256
SEND = 24
F32, BF16 = jnp.float32, jnp.bfloat16


def kernel_set(sigma_val):
    radius = 3 * sigma_val
    offsets = [float(step) for step in range(-radius, radius + 1)]
    smooth = [math.exp(-step * step / (2.0 * sigma_val**2)) for step in offsets]
    weight_total = sum(smooth)
    smooth = [value / weight_total for value in smooth]
    first_order = [step / sigma_val**2 * value for step, value in zip(offsets, smooth)]
    second = [
        (step * step / sigma_val**4 - 1.0 / sigma_val**2) * value
        for step, value in zip(offsets, smooth)
    ]
    return (radius, [smooth, first_order, second])


def banded(weights, radius, rows, columns, offset):
    matrix = np.zeros((rows, columns))
    for row in range(rows):
        for tap, weight in enumerate(weights):
            column = row + offset + tap - radius
            if 0 <= column < columns:
                matrix[row, column] = weight
    return matrix


def two_parts(matrix):
    high = matrix.astype(np.float32).astype(ml_dtypes.bfloat16)
    low = (matrix - high.astype(np.float64)).astype(np.float32).astype(ml_dtypes.bfloat16)
    return (high, low)


def filter_matrices(chunk, rows_y, width):
    along_z, along_y, along_x = ([], [], [])
    for sigma_val in SIGMAS:
        radius, filters = kernel_set(sigma_val)
        y_rows = []
        for order in range(3):
            z_matrix = banded(filters[order], radius, chunk, chunk + 2 * HALO, HALO)
            along_z.append(np.kron(z_matrix, np.eye(8)))
            y_rows.append(banded(filters[order], radius, rows_y, rows_y + 2 * HALO, HALO))
            x_matrix = banded(filters[order], radius, width, width, 0).T
            parts = np.concatenate(two_parts(x_matrix * (4.0 * sigma_val**3.5)), axis=1)
            along_x.append(np.concatenate([parts, parts], axis=0))
        y_matrix = np.concatenate(y_rows)
        y_matrix = np.pad(y_matrix, ((0, -y_matrix.shape[0] % 16), (0, 0)))
        high, low = two_parts(y_matrix)
        along_y.append(np.concatenate([high, high, low], axis=1))
    z_parts = np.concatenate(two_parts(np.concatenate(along_z)), axis=0)
    return (z_parts, np.stack(along_y), np.stack(along_x))


def split(value):
    high = value.astype(BF16)
    return (high, (value - high.astype(F32)).astype(BF16))


def filters_of(
    z_start, chunk, ext, wz_ref, wy_ref, wx_ref, z_high, z_low, y_out, channels, bands, like_ref
):
    rows_y, width = like_ref.shape[1:]
    deep = rows_y + 2 * HALO
    rows = chunk * rows_y
    piece = wz_ref.shape[0] // (2 * 6 * 8)
    planes = 6 * piece

    for first in range(0, chunk, piece):
        for pair in range(deep // 16):
            tiles = [
                ext[pl.ds(z_start + first, piece + 2 * HALO), pl.ds(16 * pair + 8 * half, 8), :]
                .reshape((piece + 2 * HALO) * 8, width)
                .astype(BF16)
                for half in range(2)
            ]
            out = jnp.dot(wz_ref[...], jnp.concatenate(tiles, axis=1), preferred_element_type=F32)
            out = (out[: planes * 8] + out[planes * 8 :]).reshape(planes, 8, 2 * width)
            out = jnp.concatenate([out[:, :, :width], out[:, :, width:]], axis=1)
            high, low = split(out.reshape(6, piece, 16, width))
            z_high[:, pl.ds(first, piece), pl.ds(16 * pair, 16), :] = high
            z_low[:, pl.ds(first, piece), pl.ds(16 * pair, 16), :] = low

    for scale in range(2):
        for order_z in range(3):
            for pair in range(chunk // 2):
                columns = []
                for half in range(2):
                    index = (scale * 3 + order_z, 2 * pair + half)
                    columns.append(
                        jnp.concatenate([z_high[index], z_low[index], z_high[index]], axis=0)
                    )
                deep_rows = jnp.concatenate(columns, axis=1)
                count = (3 - order_z) * rows_y
                out = jnp.dot(
                    wy_ref[scale, :count, :], deep_rows, preferred_element_type=F32
                )
                for order_y in range(3 - order_z):
                    component = [
                        i for i, o in enumerate(ORDERS) if o[1:] == (order_y, order_z)
                    ][0]
                    for half in range(2):
                        y_out[
                            scale * 6 + component, pl.ds((2 * pair + half) * rows_y, rows_y), :
                        ] = out[
                            order_y * rows_y : (order_y + 1) * rows_y,
                            half * width : (half + 1) * width,
                        ]

    tubes = []
    for scale in range(2):
        hessian = [None] * 6
        for order_x in range(3):
            members = [i for i, o in enumerate(ORDERS) if o[0] == order_x]
            two = [jnp.concatenate(split(y_out[scale * 6 + i]), axis=1) for i in members]
            out = jnp.dot(
                jnp.concatenate(two, axis=0),
                wx_ref[scale * 3 + order_x],
                preferred_element_type=F32,
            )
            out = out[:, :width] + out[:, width:]
            for index, member in enumerate(members):
                hessian[member] = out[index * rows : (index + 1) * rows]
        xx, yy, zz, xy, xz, yz = hessian
        trace = xx + yy + zz
        frob = xx * xx + yy * yy + zz * zz + 2.0 * (xy * xy + xz * xz + yz * yz)
        minors = 0.5 * (trace * trace - frob)
        tube = jnp.maximum(-trace, 0.0) * jnp.maximum(minors, 0.0) / (frob + 0.25)
        tubes.append(tube)
        for index, value in enumerate(hessian + [minors, tube]):
            channels[pl.ds((scale * 8 + index) * rows, rows), :] = value
    like = jnp.maximum(tubes[0], tubes[1])
    like_ref[pl.ds(z_start, chunk)] = like.reshape(chunk, rows_y, width).astype(BF16)

    volume = ext[pl.ds(z_start + HALO, chunk), pl.ds(HALO, rows_y), :].reshape(rows, width)
    for index, center in enumerate(CENTERS):
        bands[pl.ds(index * rows, rows), :] = jnp.exp(-((volume - center) ** 2))


def add_sums(z_start, chunk, planes, labels_ref, channels, bands, acc):
    rows_y, width = labels_ref.shape[1:]
    rows = chunk * rows_y
    group = planes * rows_y
    low_ids = lax.broadcasted_iota(jnp.int32, (LO, width), 0).astype(F32).astype(BF16)

    def step(part, carry):
        left, right = ([], [])
        marks = labels_ref[pl.ds(z_start + part * planes, planes)].reshape(group, width)
        mark_high = (marks >> 8).astype(F32)
        mark_low = (marks & 255).astype(F32)
        for row in range(group):
            at = part * group + row
            feats = []
            for scale in range(2):
                base = channels[pl.ds(scale * 8 * rows + at, 8, stride=rows), :]
                for band in range(4):
                    feats.append(base * bands[pl.ds(band * rows + at, 1), :])
            feats = jnp.concatenate(feats, axis=0).astype(BF16)
            high_of = jnp.broadcast_to(mark_high[row : row + 1], (FEAT, width)).astype(BF16)
            low_of = jnp.broadcast_to(mark_low[row : row + 1], (LO, width)).astype(BF16)
            zero = jnp.zeros_like(feats)
            left.append(
                jnp.concatenate(
                    [jnp.where(high_of == jnp.asarray(h, BF16), feats, zero) for h in range(HI)],
                    axis=0,
                )
            )
            right.append(
                jnp.where(low_of == low_ids, jnp.asarray(1, BF16), jnp.asarray(0, BF16))
            )
        acc[...] += lax.dot_general(
            jnp.concatenate(left, axis=1),
            jnp.concatenate(right, axis=1),
            (((1,), (1,)), ((), ())),
            preferred_element_type=F32,
        )
        return carry

    lax.fori_loop(0, chunk // planes, step, 0)


def all_chunks(
    start_of, count, chunk, planes, ext, labels_ref, weights, passes, buffers, acc, like_ref,
    beside=lambda index: None,
):
    def step(index, carry):
        z_start = start_of(index)
        filters_of(z_start, chunk, ext, *weights, *passes, *buffers, like_ref)
        beside(index)
        add_sums(z_start, chunk, planes, labels_ref, *buffers, acc)
        return carry

    lax.fori_loop(0, count, step, 0)


def inner_kernel(
    own_ref, labels_ref, wz_ref, wy_ref, wx_ref,
    like_ref, acc,
    ext, z_high, z_low, y_out, channels, bands,
):
    slab_z = labels_ref.shape[0]
    ext[pl.ds(HALO, slab_z)] = own_ref[...].astype(F32)
    acc[...] = jnp.zeros_like(acc)
    all_chunks(
        lambda index: HALO + index * ZC_IN, (slab_z - 2 * HALO) // ZC_IN, ZC_IN, PLANES_IN, ext, labels_ref,
        (wz_ref, wy_ref, wx_ref), (z_high, z_low, y_out),
        (channels, bands), acc, like_ref,
    )


def outer_kernel(
    owner_ref, rank_ref, ends_ref, before_ref, own_ref, after_ref, labels_ref, wz_ref, wy_ref,
    wx_ref, inner_like_ref, inner_acc_ref,
    like_ref, send_ref,
    ext, z_high, z_low, y_out, channels, bands, acc, turned, like, like_sems,
):
    slab_z = labels_ref.shape[0]
    ext[pl.ds(HALO, slab_z)] = own_ref[...].astype(F32)
    for end, (ref, at) in enumerate(((before_ref, 0), (after_ref, HALO + slab_z))):
        ext[pl.ds(at, HALO)] = jnp.where(ends_ref[end] != 0, 0.0, ref[...].astype(F32))
    acc[...] = inner_acc_ref[...]
    inner = pl.ds(HALO, slab_z - 2 * HALO)
    half = HALO // ZC_OUT
    count = 2 * half
    share = send_ref.shape[0] // count
    inner_copy = pltpu.make_async_copy(
        inner_like_ref.at[inner], like_ref.at[inner], like_sems.at[count]
    )
    inner_copy.start()

    def start_of(index):
        return index * ZC_OUT + jnp.where(index >= half, slab_z - 2 * HALO, 0)

    def like_copy(index):
        planes = pl.ds(start_of(index), ZC_OUT)
        return pltpu.make_async_copy(like.at[planes], like_ref.at[planes], like_sems.at[index])

    def beside(index):
        send_ref[pl.ds(index * share, share)] = jnp.zeros((share, *send_ref.shape[1:]), BF16)
        like_copy(index).start()

    all_chunks(
        start_of, count, ZC_OUT, PLANES_OUT, ext, labels_ref,
        (wz_ref, wy_ref, wx_ref), (z_high, z_low, y_out),
        (channels, bands), acc, like, beside,
    )

    for slot in range(owner_ref.shape[0]):
        owner = owner_ref[slot]
        rank = rank_ref[slot].astype(F32)
        for scale in range(2):
            for band in range(4):
                turned[pl.ds(32 * scale + band, 8, stride=4), :] = acc[
                    pl.ds((slot // 2) * FEAT + 32 * scale + 8 * band, 8),
                    pl.ds((slot % 2) * LBL, LBL),
                ]
        for quarter in range(4):
            send_ref[owner, quarter, pl.ds(0, 16), :] = turned[pl.ds(16 * quarter, 16), :].astype(
                BF16
            )
            send_ref[owner, quarter, pl.ds(16, 8), :] = jnp.full((8, LBL), rank, F32).astype(BF16)
    for index in range(count):
        like_copy(index).wait()
    inner_copy.wait()


def sum_kernel(got_ref, out_ref):
    sources = got_ref.shape[0]

    def step(source, totals):
        block = got_ref[source].astype(F32)
        data, rank = (block[:16], jnp.concatenate([block[16:], block[16:]], axis=0))
        return tuple(
            total + jnp.where(rank == float(index), data, 0.0) for index, total in enumerate(totals)
        )

    totals = lax.fori_loop(
        0,
        sources,
        step,
        tuple(jnp.zeros(out_ref.shape[1:], F32) for _ in range(out_ref.shape[0])),
        unroll=8,
    )
    for index, total in enumerate(totals):
        out_ref[index] = total


def neighbours(shard, axis, dim, width):
    size, length = (lax.axis_size(axis), shard.shape[dim])
    up = [(i, (i + 1) % size) for i in range(size)]
    down = [(j, i) for i, j in up]
    last = lax.slice_in_dim(shard, length - width, length, axis=dim)
    leading = lax.slice_in_dim(shard, 0, width, axis=dim)
    here = lax.axis_index(axis)
    ends = (here == 0, here == size - 1)
    return (lax.ppermute(last, axis, up), lax.ppermute(leading, axis, down), ends)


VMEM = pl.BlockSpec(memory_space=pltpu.VMEM)
SMEM = pl.BlockSpec(memory_space=pltpu.SMEM)


def scratch(chunk, slab_z, rows_y, width):
    rows = chunk * rows_y
    deep = rows_y + 2 * HALO
    return [
        pltpu.VMEM((slab_z + 2 * HALO, deep, width), F32),
        pltpu.VMEM((6, chunk, deep, width), BF16),
        pltpu.VMEM((6, chunk, deep, width), BF16),
        pltpu.VMEM((12, rows, width), F32),
        pltpu.VMEM((16 * rows, width), F32),
        pltpu.VMEM((4 * rows, width), F32),
    ]


def cost(share):
    return pl.CostEstimate(
        flops=int(share * 28e9), bytes_accessed=int(share * 4e6), transcendentals=int(share * 4e5)
    )


PARAMS = pltpu.CompilerParams(vmem_limit_bytes=36 * 1024 * 1024)


def inner_sums(own, labels):
    matrices = filter_matrices(ZP_IN, *labels.shape[1:])
    return pl.pallas_call(
        inner_kernel,
        out_shape=(
            jax.ShapeDtypeStruct(labels.shape, BF16),
            jax.ShapeDtypeStruct((HI * FEAT, LO), F32),
        ),
        in_specs=[VMEM] * 5,
        out_specs=(VMEM, VMEM),
        scratch_shapes=scratch(ZC_IN, *labels.shape),
        compiler_params=PARAMS,
        cost_estimate=cost(0.25),
    )(own, labels, *matrices)


def outer_sums(owners, ranks, ends, before, own, after, labels, inner, groups, quarters):
    matrices = filter_matrices(ZP_OUT, *labels.shape[1:])
    return pl.pallas_call(
        outer_kernel,
        out_shape=(
            jax.ShapeDtypeStruct(labels.shape, BF16),
            jax.ShapeDtypeStruct((groups, quarters, SEND, LBL), BF16),
        ),
        in_specs=[SMEM] * 3 + [VMEM] * 9,
        out_specs=(pl.BlockSpec(memory_space=pl.ANY), VMEM),
        scratch_shapes=scratch(ZC_OUT, *labels.shape)
        + [
            pltpu.VMEM((HI * FEAT, LO), F32),
            pltpu.VMEM((FEAT, LBL), F32),
            pltpu.VMEM(labels.shape, BF16),
            pltpu.SemaphoreType.DMA((2 * HALO // ZC_OUT + 1,)),
        ],
        compiler_params=PARAMS,
        cost_estimate=cost(0.75),
    )(owners, ranks, ends, before, own, after, labels, *matrices, *inner)


def local(image, labels, brick_blocks, block_owner):
    groups = lax.axis_size("gy")
    quarters = lax.axis_size("gz")
    listed_count = brick_blocks.shape[-1]
    total_blocks = block_owner.shape[0]
    blk_dev = total_blocks // groups
    block_index = jnp.arange(total_blocks, dtype=jnp.int32)
    earlier = (block_index[None, :] < block_index[:, None]) & (
        block_owner[None, :] == block_owner[:, None]
    )
    owner_rank = jnp.sum(earlier.astype(jnp.int32), axis=1)
    listed_ids = brick_blocks.reshape(listed_count)
    listed = (listed_ids[:, None] == block_index[None, :]).astype(jnp.int32)
    owners = jnp.sum(listed * block_owner[None, :], axis=1)
    ranks = jnp.sum(listed * owner_rank[None, :], axis=1)

    left, right, (first, last) = neighbours(image, "gy", 1, HALO)
    zero = jnp.zeros((), image.dtype)
    own = jnp.concatenate(
        [jnp.where(first, zero, left), image, jnp.where(last, zero, right)], axis=1
    )
    before, after, ends = neighbours(own, "gz", 0, HALO)
    inner = inner_sums(own, labels)
    likeness, message = outer_sums(
        owners, ranks, jnp.stack(ends).astype(jnp.int32), before, own, after, labels, inner,
        groups, quarters,
    )
    message = message.reshape(groups * quarters, SEND, LBL)
    got = lax.all_to_all(message, ("gy", "gz"), 0, 0, tiled=True)
    label_features = pl.pallas_call(
        sum_kernel,
        out_shape=jax.ShapeDtypeStruct((blk_dev, FEAT // quarters, LBL), F32),
        compiler_params=pltpu.CompilerParams(vmem_limit_bytes=6 * 1024 * 1024),
    )(got)
    return (likeness, label_features)


def solution(mesh):
    placed = (P("gz", "gy", None), P("gz", "gy", None), P("gz", "gy", None), P())
    return jax.shard_map(
        local,
        mesh=mesh,
        in_specs=placed,
        out_specs=(P("gz", "gy", None), P("gy", "gz", None)),
        check_vma=False,
    )
```

```python
import math

import jax
import jax.numpy as jnp
import ml_dtypes
import numpy as np
from jax import lax
from jax.experimental import pallas as pl
from jax.experimental.pallas import tpu as pltpu
from jax.sharding import PartitionSpec as P

LBL = 128
FEAT = 64
HALO = 12
ZC_IN, ZC_OUT = (8, 12)
ZP_IN, ZP_OUT = (8, 6)
PLANES_IN, PLANES_OUT = (4, 6)
SIGMAS = (2, 4)
CENTERS = (-1.5, -0.5, 0.5, 1.5)
ORDERS = ((2, 0, 0), (0, 2, 0), (0, 0, 2), (1, 1, 0), (1, 0, 1), (0, 1, 1))
HI = 8
LO = 256
SEND = 24
F32, BF16 = jnp.float32, jnp.bfloat16


def kernel_set(sigma_val):
    radius = 3 * sigma_val
    offsets = [float(step) for step in range(-radius, radius + 1)]
    smooth = [math.exp(-step * step / (2.0 * sigma_val**2)) for step in offsets]
    weight_total = sum(smooth)
    smooth = [value / weight_total for value in smooth]
    first_order = [step / sigma_val**2 * value for step, value in zip(offsets, smooth)]
    second = [
        (step * step / sigma_val**4 - 1.0 / sigma_val**2) * value
        for step, value in zip(offsets, smooth)
    ]
    return (radius, [smooth, first_order, second])


def banded(weights, radius, rows, columns, offset):
    matrix = np.zeros((rows, columns))
    for row in range(rows):
        for tap, weight in enumerate(weights):
            column = row + offset + tap - radius
            if 0 <= column < columns:
                matrix[row, column] = weight
    return matrix


def two_parts(matrix):
    high = matrix.astype(np.float32).astype(ml_dtypes.bfloat16)
    low = (matrix - high.astype(np.float64)).astype(np.float32).astype(ml_dtypes.bfloat16)
    return (high, low)


def filter_matrices(chunk, rows_y, width):
    along_z, along_y, along_x = ([], [], [])
    for sigma_val in SIGMAS:
        radius, filters = kernel_set(sigma_val)
        y_rows = []
        for order in range(3):
            z_matrix = banded(filters[order], radius, chunk, chunk + 2 * HALO, HALO)
            along_z.append(np.kron(z_matrix, np.eye(8)))
            y_rows.append(banded(filters[order], radius, rows_y, rows_y + 2 * HALO, HALO))
            x_matrix = banded(filters[order], radius, width, width, 0).T
            parts = np.concatenate(two_parts(x_matrix * (4.0 * sigma_val**3.5)), axis=1)
            along_x.append(np.concatenate([parts, parts], axis=0))
        y_matrix = np.concatenate(y_rows)
        y_matrix = np.pad(y_matrix, ((0, -y_matrix.shape[0] % 16), (0, 0)))
        high, low = two_parts(y_matrix)
        along_y.append(np.concatenate([high, high, low], axis=1))
    z_parts = np.concatenate(two_parts(np.concatenate(along_z)), axis=0)
    return (z_parts, np.stack(along_y), np.stack(along_x))


def split(value):
    high = value.astype(BF16)
    return (high, (value - high.astype(F32)).astype(BF16))


def filters_of(
    z_start, chunk, ext, wz_ref, wy_ref, wx_ref, z_high, z_low, y_out, channels, bands, like_ref
):
    rows_y, width = like_ref.shape[1:]
    deep = rows_y + 2 * HALO
    rows = chunk * rows_y
    piece = wz_ref.shape[0] // (2 * 6 * 8)
    planes = 6 * piece

    for first in range(0, chunk, piece):
        for pair in range(deep // 16):
            tiles = [
                ext[pl.ds(z_start + first, piece + 2 * HALO), pl.ds(16 * pair + 8 * half, 8), :]
                .reshape((piece + 2 * HALO) * 8, width)
                .astype(BF16)
                for half in range(2)
            ]
            out = jnp.dot(wz_ref[...], jnp.concatenate(tiles, axis=1), preferred_element_type=F32)
            out = (out[: planes * 8] + out[planes * 8 :]).reshape(planes, 8, 2 * width)
            out = jnp.concatenate([out[:, :, :width], out[:, :, width:]], axis=1)
            high, low = split(out.reshape(6, piece, 16, width))
            z_high[:, pl.ds(first, piece), pl.ds(16 * pair, 16), :] = high
            z_low[:, pl.ds(first, piece), pl.ds(16 * pair, 16), :] = low

    for scale in range(2):
        for order_z in range(3):
            for pair in range(chunk // 2):
                columns = []
                for half in range(2):
                    index = (scale * 3 + order_z, 2 * pair + half)
                    columns.append(
                        jnp.concatenate([z_high[index], z_low[index], z_high[index]], axis=0)
                    )
                deep_rows = jnp.concatenate(columns, axis=1)
                count = (3 - order_z) * rows_y
                out = jnp.dot(
                    wy_ref[scale, :count, :], deep_rows, preferred_element_type=F32
                )
                for order_y in range(3 - order_z):
                    component = [
                        i for i, o in enumerate(ORDERS) if o[1:] == (order_y, order_z)
                    ][0]
                    for half in range(2):
                        y_out[
                            scale * 6 + component, pl.ds((2 * pair + half) * rows_y, rows_y), :
                        ] = out[
                            order_y * rows_y : (order_y + 1) * rows_y,
                            half * width : (half + 1) * width,
                        ]

    tubes = []
    for scale in range(2):
        hessian = [None] * 6
        for order_x in range(3):
            members = [i for i, o in enumerate(ORDERS) if o[0] == order_x]
            two = [jnp.concatenate(split(y_out[scale * 6 + i]), axis=1) for i in members]
            out = jnp.dot(
                jnp.concatenate(two, axis=0),
                wx_ref[scale * 3 + order_x],
                preferred_element_type=F32,
            )
            out = out[:, :width] + out[:, width:]
            for index, member in enumerate(members):
                hessian[member] = out[index * rows : (index + 1) * rows]
        xx, yy, zz, xy, xz, yz = hessian
        trace = xx + yy + zz
        frob = xx * xx + yy * yy + zz * zz + 2.0 * (xy * xy + xz * xz + yz * yz)
        minors = 0.5 * (trace * trace - frob)
        tube = jnp.maximum(-trace, 0.0) * jnp.maximum(minors, 0.0) / (frob + 0.25)
        tubes.append(tube)
        for index, value in enumerate(hessian + [minors, tube]):
            channels[pl.ds((scale * 8 + index) * rows, rows), :] = value
    like = jnp.maximum(tubes[0], tubes[1])
    like_ref[pl.ds(z_start, chunk)] = like.reshape(chunk, rows_y, width).astype(BF16)

    volume = ext[pl.ds(z_start + HALO, chunk), pl.ds(HALO, rows_y), :].reshape(rows, width)
    for index, center in enumerate(CENTERS):
        bands[pl.ds(index * rows, rows), :] = jnp.exp(-((volume - center) ** 2))


def add_sums(z_start, chunk, planes, labels_ref, channels, bands, acc):
    rows_y, width = labels_ref.shape[1:]
    rows = chunk * rows_y
    group = planes * rows_y
    low_ids = lax.broadcasted_iota(jnp.int32, (LO, width), 0).astype(F32).astype(BF16)

    def step(part, carry):
        left, right = ([], [])
        marks = labels_ref[pl.ds(z_start + part * planes, planes)].reshape(group, width)
        mark_high = (marks >> 8).astype(F32)
        mark_low = (marks & 255).astype(F32)
        for row in range(group):
            at = part * group + row
            feats = []
            for scale in range(2):
                base = channels[pl.ds(scale * 8 * rows + at, 8, stride=rows), :]
                for band in range(4):
                    feats.append(base * bands[pl.ds(band * rows + at, 1), :])
            feats = jnp.concatenate(feats, axis=0).astype(BF16)
            high_of = jnp.broadcast_to(mark_high[row : row + 1], (FEAT, width)).astype(BF16)
            low_of = jnp.broadcast_to(mark_low[row : row + 1], (LO, width)).astype(BF16)
            zero = jnp.zeros_like(feats)
            left.append(
                jnp.concatenate(
                    [jnp.where(high_of == jnp.asarray(h, BF16), feats, zero) for h in range(HI)],
                    axis=0,
                )
            )
            right.append(
                jnp.where(low_of == low_ids, jnp.asarray(1, BF16), jnp.asarray(0, BF16))
            )
        acc[...] += lax.dot_general(
            jnp.concatenate(left, axis=1),
            jnp.concatenate(right, axis=1),
            (((1,), (1,)), ((), ())),
            preferred_element_type=F32,
        )
        return carry

    lax.fori_loop(0, chunk // planes, step, 0)


def all_chunks(
    start_of, count, chunk, planes, ext, labels_ref, weights, passes, buffers, acc, like_ref,
    beside=lambda index: None,
):
    def step(index, carry):
        z_start = start_of(index)
        filters_of(z_start, chunk, ext, *weights, *passes, *buffers, like_ref)
        beside(index)
        add_sums(z_start, chunk, planes, labels_ref, *buffers, acc)
        return carry

    lax.fori_loop(0, count, step, 0)


def inner_kernel(
    own_ref, labels_ref, wz_ref, wy_ref, wx_ref,
    like_ref, acc,
    ext, z_high, z_low, y_out, channels, bands,
):
    slab_z = labels_ref.shape[0]
    ext[pl.ds(HALO, slab_z)] = own_ref[...].astype(F32)
    acc[...] = jnp.zeros_like(acc)
    all_chunks(
        lambda index: HALO + index * ZC_IN, (slab_z - 2 * HALO) // ZC_IN, ZC_IN, PLANES_IN, ext, labels_ref,
        (wz_ref, wy_ref, wx_ref), (z_high, z_low, y_out),
        (channels, bands), acc, like_ref,
    )


def outer_kernel(
    owner_ref, rank_ref, ends_ref, before_ref, own_ref, after_ref, labels_ref, wz_ref, wy_ref,
    wx_ref, inner_like_ref, inner_acc_ref,
    like_ref, send_ref,
    ext, z_high, z_low, y_out, channels, bands, acc, turned, like, like_sems,
):
    slab_z = labels_ref.shape[0]
    ext[pl.ds(HALO, slab_z)] = own_ref[...].astype(F32)
    for end, (ref, at) in enumerate(((before_ref, 0), (after_ref, HALO + slab_z))):
        ext[pl.ds(at, HALO)] = jnp.where(ends_ref[end] != 0, 0.0, ref[...].astype(F32))
    acc[...] = inner_acc_ref[...]
    inner = pl.ds(HALO, slab_z - 2 * HALO)
    half = HALO // ZC_OUT
    count = 2 * half
    share = send_ref.shape[0] // count
    inner_copy = pltpu.make_async_copy(
        inner_like_ref.at[inner], like_ref.at[inner], like_sems.at[count]
    )
    inner_copy.start()

    def start_of(index):
        return index * ZC_OUT + jnp.where(index >= half, slab_z - 2 * HALO, 0)

    def like_copy(index):
        planes = pl.ds(start_of(index), ZC_OUT)
        return pltpu.make_async_copy(like.at[planes], like_ref.at[planes], like_sems.at[index])

    def beside(index):
        send_ref[pl.ds(index * share, share)] = jnp.zeros((share, *send_ref.shape[1:]), BF16)
        like_copy(index).start()

    all_chunks(
        start_of, count, ZC_OUT, PLANES_OUT, ext, labels_ref,
        (wz_ref, wy_ref, wx_ref), (z_high, z_low, y_out),
        (channels, bands), acc, like, beside,
    )

    for slot in range(owner_ref.shape[0]):
        owner = owner_ref[slot]
        rank = rank_ref[slot].astype(F32)
        for scale in range(2):
            for band in range(4):
                turned[pl.ds(32 * scale + band, 8, stride=4), :] = acc[
                    pl.ds((slot // 2) * FEAT + 32 * scale + 8 * band, 8),
                    pl.ds((slot % 2) * LBL, LBL),
                ]
        for quarter in range(4):
            send_ref[owner, quarter, pl.ds(0, 16), :] = turned[pl.ds(16 * quarter, 16), :].astype(
                BF16
            )
            send_ref[owner, quarter, pl.ds(16, 8), :] = jnp.full((8, LBL), rank, F32).astype(BF16)
    for index in range(count):
        like_copy(index).wait()
    inner_copy.wait()


def sum_kernel(got_ref, out_ref):
    sources = got_ref.shape[0]

    def step(source, totals):
        block = got_ref[source].astype(F32)
        data, rank = (block[:16], jnp.concatenate([block[16:], block[16:]], axis=0))
        return tuple(
            total + jnp.where(rank == float(index), data, 0.0) for index, total in enumerate(totals)
        )

    totals = lax.fori_loop(
        0,
        sources,
        step,
        tuple(jnp.zeros(out_ref.shape[1:], F32) for _ in range(out_ref.shape[0])),
        unroll=8,
    )
    for index, total in enumerate(totals):
        out_ref[index] = total


def neighbours(shard, axis, dim, width):
    size, length = (lax.axis_size(axis), shard.shape[dim])
    up = [(i, (i + 1) % size) for i in range(size)]
    down = [(j, i) for i, j in up]
    last = lax.slice_in_dim(shard, length - width, length, axis=dim)
    leading = lax.slice_in_dim(shard, 0, width, axis=dim)
    here = lax.axis_index(axis)
    ends = (here == 0, here == size - 1)
    return (lax.ppermute(last, axis, up), lax.ppermute(leading, axis, down), ends)


def paired_neighbours(shard, axis, dim, width):
    size, length = (lax.axis_size(axis), shard.shape[dim])
    here = lax.axis_index(axis)
    odd = here % 2 == 1
    last = lax.slice_in_dim(shard, length - width, length, axis=dim)
    leading = lax.slice_in_dim(shard, 0, width, axis=dim)
    outer = [(i, (i + 1) % size if i % 2 else (i - 1) % size) for i in range(size)]
    inner = [(i, i ^ 1) for i in range(size)]
    from_outer = lax.ppermute(jnp.where(odd, last, leading), axis, outer)
    from_inner = lax.ppermute(jnp.where(odd, leading, last), axis, inner)
    before = jnp.where(odd, from_inner, from_outer)
    after = jnp.where(odd, from_outer, from_inner)
    return (before, after, (here == 0, here == size - 1))


VMEM = pl.BlockSpec(memory_space=pltpu.VMEM)
SMEM = pl.BlockSpec(memory_space=pltpu.SMEM)


def scratch(chunk, slab_z, rows_y, width):
    rows = chunk * rows_y
    deep = rows_y + 2 * HALO
    return [
        pltpu.VMEM((slab_z + 2 * HALO, deep, width), F32),
        pltpu.VMEM((6, chunk, deep, width), BF16),
        pltpu.VMEM((6, chunk, deep, width), BF16),
        pltpu.VMEM((12, rows, width), F32),
        pltpu.VMEM((16 * rows, width), F32),
        pltpu.VMEM((4 * rows, width), F32),
    ]


def cost(share):
    return pl.CostEstimate(
        flops=int(share * 28e9), bytes_accessed=int(share * 4e6), transcendentals=int(share * 4e5)
    )


PARAMS = pltpu.CompilerParams(vmem_limit_bytes=36 * 1024 * 1024)


def inner_sums(own, labels):
    matrices = filter_matrices(ZP_IN, *labels.shape[1:])
    return pl.pallas_call(
        inner_kernel,
        out_shape=(
            jax.ShapeDtypeStruct(labels.shape, BF16),
            jax.ShapeDtypeStruct((HI * FEAT, LO), F32),
        ),
        in_specs=[VMEM] * 5,
        out_specs=(VMEM, VMEM),
        scratch_shapes=scratch(ZC_IN, *labels.shape),
        compiler_params=PARAMS,
        cost_estimate=cost(0.25),
    )(own, labels, *matrices)


def outer_sums(owners, ranks, ends, before, own, after, labels, inner, groups, quarters):
    matrices = filter_matrices(ZP_OUT, *labels.shape[1:])
    return pl.pallas_call(
        outer_kernel,
        out_shape=(
            jax.ShapeDtypeStruct(labels.shape, BF16),
            jax.ShapeDtypeStruct((groups, quarters, SEND, LBL), BF16),
        ),
        in_specs=[SMEM] * 3 + [VMEM] * 9,
        out_specs=(pl.BlockSpec(memory_space=pl.ANY), VMEM),
        scratch_shapes=scratch(ZC_OUT, *labels.shape)
        + [
            pltpu.VMEM((HI * FEAT, LO), F32),
            pltpu.VMEM((FEAT, LBL), F32),
            pltpu.VMEM(labels.shape, BF16),
            pltpu.SemaphoreType.DMA((2 * HALO // ZC_OUT + 1,)),
        ],
        compiler_params=PARAMS,
        cost_estimate=cost(0.75),
    )(owners, ranks, ends, before, own, after, labels, *matrices, *inner)


def local(image, labels, brick_blocks, block_owner):
    groups = lax.axis_size("gy")
    quarters = lax.axis_size("gz")
    listed_count = brick_blocks.shape[-1]
    total_blocks = block_owner.shape[0]
    blk_dev = total_blocks // groups
    block_index = jnp.arange(total_blocks, dtype=jnp.int32)
    earlier = (block_index[None, :] < block_index[:, None]) & (
        block_owner[None, :] == block_owner[:, None]
    )
    owner_rank = jnp.sum(earlier.astype(jnp.int32), axis=1)
    listed_ids = brick_blocks.reshape(listed_count)
    listed = (listed_ids[:, None] == block_index[None, :]).astype(jnp.int32)
    owners = jnp.sum(listed * block_owner[None, :], axis=1)
    ranks = jnp.sum(listed * owner_rank[None, :], axis=1)

    left, right, (first, last) = paired_neighbours(image, "gy", 1, HALO)
    zero = jnp.zeros((), image.dtype)
    own = jnp.concatenate(
        [jnp.where(first, zero, left), image, jnp.where(last, zero, right)], axis=1
    )
    before, after, ends = neighbours(own, "gz", 0, HALO)
    inner = inner_sums(own, labels)
    likeness, message = outer_sums(
        owners, ranks, jnp.stack(ends).astype(jnp.int32), before, own, after, labels, inner,
        groups, quarters,
    )
    message = message.reshape(groups * quarters, SEND, LBL)
    got = lax.all_to_all(message, ("gy", "gz"), 0, 0, tiled=True)
    label_features = pl.pallas_call(
        sum_kernel,
        out_shape=jax.ShapeDtypeStruct((blk_dev, FEAT // quarters, LBL), F32),
        compiler_params=pltpu.CompilerParams(vmem_limit_bytes=6 * 1024 * 1024),
    )(got)
    return (likeness, label_features)


def solution(mesh):
    placed = (P("gz", "gy", None), P("gz", "gy", None), P("gz", "gy", None), P())
    return jax.shard_map(
        local,
        mesh=mesh,
        in_specs=placed,
        out_specs=(P("gz", "gy", None), P("gy", "gz", None)),
        check_vma=False,
    )
```

```python
import math

import jax
import jax.numpy as jnp
import ml_dtypes
import numpy as np
from jax import lax
from jax.experimental import pallas as pl
from jax.experimental.pallas import tpu as pltpu
from jax.sharding import PartitionSpec as P

LBL = 128
FEAT = 64
HALO = 12
ZC_IN, ZC_OUT = (8, 12)
ZP_IN, ZP_OUT = (8, 6)
PLANES_IN, PLANES_OUT = (4, 6)
SIGMAS = (2, 4)
CENTERS = (-1.5, -0.5, 0.5, 1.5)
ORDERS = ((2, 0, 0), (0, 2, 0), (0, 0, 2), (1, 1, 0), (1, 0, 1), (0, 1, 1))
HI = 8
LO = 256
SEND = 5
F32, BF16 = jnp.float32, jnp.bfloat16


def kernel_set(sigma_val):
    radius = 3 * sigma_val
    offsets = [float(step) for step in range(-radius, radius + 1)]
    smooth = [math.exp(-step * step / (2.0 * sigma_val**2)) for step in offsets]
    weight_total = sum(smooth)
    smooth = [value / weight_total for value in smooth]
    first_order = [step / sigma_val**2 * value for step, value in zip(offsets, smooth)]
    second = [
        (step * step / sigma_val**4 - 1.0 / sigma_val**2) * value
        for step, value in zip(offsets, smooth)
    ]
    return (radius, [smooth, first_order, second])


def banded(weights, radius, rows, columns, offset):
    matrix = np.zeros((rows, columns))
    for row in range(rows):
        for tap, weight in enumerate(weights):
            column = row + offset + tap - radius
            if 0 <= column < columns:
                matrix[row, column] = weight
    return matrix


def two_parts(matrix):
    high = matrix.astype(np.float32).astype(ml_dtypes.bfloat16)
    low = (matrix - high.astype(np.float64)).astype(np.float32).astype(ml_dtypes.bfloat16)
    return (high, low)


def filter_matrices(chunk, rows_y, width):
    along_z, along_y, along_x = ([], [], [])
    for sigma_val in SIGMAS:
        radius, filters = kernel_set(sigma_val)
        y_rows = []
        for order in range(3):
            z_matrix = banded(filters[order], radius, chunk, chunk + 2 * HALO, HALO)
            along_z.append(np.kron(z_matrix, np.eye(8)))
            y_rows.append(banded(filters[order], radius, rows_y, rows_y + 2 * HALO, HALO))
            x_matrix = banded(filters[order], radius, width, width, 0).T
            parts = np.concatenate(two_parts(x_matrix * (4.0 * sigma_val**3.5)), axis=1)
            along_x.append(np.concatenate([parts, parts], axis=0))
        y_matrix = np.concatenate(y_rows)
        y_matrix = np.pad(y_matrix, ((0, -y_matrix.shape[0] % 16), (0, 0)))
        high, low = two_parts(y_matrix)
        along_y.append(np.concatenate([high, high, low], axis=1))
    z_parts = np.concatenate(two_parts(np.concatenate(along_z)), axis=0)
    return (z_parts, np.stack(along_y), np.stack(along_x))


def split(value):
    high = value.astype(BF16)
    return (high, (value - high.astype(F32)).astype(BF16))


def filters_of(
    z_start, chunk, ext, wz_ref, wy_ref, wx_ref, z_high, z_low, y_out, channels, bands, like_ref
):
    rows_y, width = like_ref.shape[1:]
    deep = rows_y + 2 * HALO
    rows = chunk * rows_y
    piece = wz_ref.shape[0] // (2 * 6 * 8)
    planes = 6 * piece

    for first in range(0, chunk, piece):
        for pair in range(deep // 16):
            tiles = [
                ext[pl.ds(z_start + first, piece + 2 * HALO), pl.ds(16 * pair + 8 * half, 8), :]
                .reshape((piece + 2 * HALO) * 8, width)
                .astype(BF16)
                for half in range(2)
            ]
            out = jnp.dot(wz_ref[...], jnp.concatenate(tiles, axis=1), preferred_element_type=F32)
            out = (out[: planes * 8] + out[planes * 8 :]).reshape(planes, 8, 2 * width)
            out = jnp.concatenate([out[:, :, :width], out[:, :, width:]], axis=1)
            high, low = split(out.reshape(6, piece, 16, width))
            z_high[:, pl.ds(first, piece), pl.ds(16 * pair, 16), :] = high
            z_low[:, pl.ds(first, piece), pl.ds(16 * pair, 16), :] = low

    for scale in range(2):
        for order_z in range(3):
            for pair in range(chunk // 2):
                columns = []
                for half in range(2):
                    index = (scale * 3 + order_z, 2 * pair + half)
                    columns.append(
                        jnp.concatenate([z_high[index], z_low[index], z_high[index]], axis=0)
                    )
                deep_rows = jnp.concatenate(columns, axis=1)
                count = (3 - order_z) * rows_y
                out = jnp.dot(
                    wy_ref[scale, :count, :], deep_rows, preferred_element_type=F32
                )
                for order_y in range(3 - order_z):
                    component = [
                        i for i, o in enumerate(ORDERS) if o[1:] == (order_y, order_z)
                    ][0]
                    for half in range(2):
                        y_out[
                            scale * 6 + component, pl.ds((2 * pair + half) * rows_y, rows_y), :
                        ] = out[
                            order_y * rows_y : (order_y + 1) * rows_y,
                            half * width : (half + 1) * width,
                        ]

    tubes = []
    for scale in range(2):
        hessian = [None] * 6
        for order_x in range(3):
            members = [i for i, o in enumerate(ORDERS) if o[0] == order_x]
            two = [jnp.concatenate(split(y_out[scale * 6 + i]), axis=1) for i in members]
            out = jnp.dot(
                jnp.concatenate(two, axis=0),
                wx_ref[scale * 3 + order_x],
                preferred_element_type=F32,
            )
            out = out[:, :width] + out[:, width:]
            for index, member in enumerate(members):
                hessian[member] = out[index * rows : (index + 1) * rows]
        xx, yy, zz, xy, xz, yz = hessian
        trace = xx + yy + zz
        frob = xx * xx + yy * yy + zz * zz + 2.0 * (xy * xy + xz * xz + yz * yz)
        minors = 0.5 * (trace * trace - frob)
        tube = jnp.maximum(-trace, 0.0) * jnp.maximum(minors, 0.0) / (frob + 0.25)
        tubes.append(tube)
        for index, value in enumerate(hessian + [minors, tube]):
            channels[pl.ds((scale * 8 + index) * rows, rows), :] = value
    like = jnp.maximum(tubes[0], tubes[1])
    like_ref[pl.ds(z_start, chunk)] = like.reshape(chunk, rows_y, width).astype(BF16)

    volume = ext[pl.ds(z_start + HALO, chunk), pl.ds(HALO, rows_y), :].reshape(rows, width)
    for index, center in enumerate(CENTERS):
        bands[pl.ds(index * rows, rows), :] = jnp.exp(-((volume - center) ** 2))


def add_sums(z_start, chunk, planes, labels_ref, channels, bands, acc):
    rows_y, width = labels_ref.shape[1:]
    rows = chunk * rows_y
    group = planes * rows_y
    low_ids = lax.broadcasted_iota(jnp.int32, (LO, width), 0).astype(F32).astype(BF16)

    def step(part, carry):
        left, right = ([], [])
        marks = labels_ref[pl.ds(z_start + part * planes, planes)].reshape(group, width)
        mark_high = (marks >> 8).astype(F32)
        mark_low = (marks & 255).astype(F32)
        for row in range(group):
            at = part * group + row
            feats = []
            for scale in range(2):
                base = channels[pl.ds(scale * 8 * rows + at, 8, stride=rows), :]
                for band in range(4):
                    feats.append(base * bands[pl.ds(band * rows + at, 1), :])
            feats = jnp.concatenate(feats, axis=0).astype(BF16)
            high_of = jnp.broadcast_to(mark_high[row : row + 1], (FEAT, width)).astype(BF16)
            low_of = jnp.broadcast_to(mark_low[row : row + 1], (LO, width)).astype(BF16)
            zero = jnp.zeros_like(feats)
            left.append(
                jnp.concatenate(
                    [jnp.where(high_of == jnp.asarray(h, BF16), feats, zero) for h in range(HI)],
                    axis=0,
                )
            )
            right.append(
                jnp.where(low_of == low_ids, jnp.asarray(1, BF16), jnp.asarray(0, BF16))
            )
        acc[...] += lax.dot_general(
            jnp.concatenate(left, axis=1),
            jnp.concatenate(right, axis=1),
            (((1,), (1,)), ((), ())),
            preferred_element_type=F32,
        )
        return carry

    lax.fori_loop(0, chunk // planes, step, 0)


def all_chunks(
    start_of, count, chunk, planes, ext, labels_ref, weights, passes, buffers, acc, like_ref,
    beside=lambda index: None,
):
    def step(index, carry):
        z_start = start_of(index)
        filters_of(z_start, chunk, ext, *weights, *passes, *buffers, like_ref)
        beside(index)
        add_sums(z_start, chunk, planes, labels_ref, *buffers, acc)
        return carry

    lax.fori_loop(0, count, step, 0)


def inner_kernel(
    own_ref, labels_ref, wz_ref, wy_ref, wx_ref,
    like_ref, acc,
    ext, z_high, z_low, y_out, channels, bands,
):
    slab_z = labels_ref.shape[0]
    ext[pl.ds(HALO, slab_z)] = own_ref[...].astype(F32)
    acc[...] = jnp.zeros_like(acc)
    all_chunks(
        lambda index: HALO + index * ZC_IN, (slab_z - 2 * HALO) // ZC_IN, ZC_IN, PLANES_IN, ext, labels_ref,
        (wz_ref, wy_ref, wx_ref), (z_high, z_low, y_out),
        (channels, bands), acc, like_ref,
    )


def outer_kernel(
    owner_ref, rank_ref, ends_ref, before_ref, own_ref, after_ref, labels_ref, wz_ref, wy_ref,
    wx_ref, inner_like_ref, inner_acc_ref,
    like_ref, send_ref,
    ext, z_high, z_low, y_out, channels, bands, acc, turned, like, like_sems,
):
    slab_z = labels_ref.shape[0]
    ext[pl.ds(HALO, slab_z)] = own_ref[...].astype(F32)
    for end, (ref, at) in enumerate(((before_ref, 0), (after_ref, HALO + slab_z))):
        ext[pl.ds(at, HALO)] = jnp.where(ends_ref[end] != 0, 0.0, ref[...].astype(F32))
    acc[...] = inner_acc_ref[...]
    inner = pl.ds(HALO, slab_z - 2 * HALO)
    half = HALO // ZC_OUT
    count = 2 * half
    share = send_ref.shape[0] // count
    inner_copy = pltpu.make_async_copy(
        inner_like_ref.at[inner], like_ref.at[inner], like_sems.at[count]
    )
    inner_copy.start()

    def start_of(index):
        return index * ZC_OUT + jnp.where(index >= half, slab_z - 2 * HALO, 0)

    def like_copy(index):
        planes = pl.ds(start_of(index), ZC_OUT)
        return pltpu.make_async_copy(like.at[planes], like_ref.at[planes], like_sems.at[index])

    def beside(index):
        send_ref[pl.ds(index * share, share)] = jnp.zeros((share, *send_ref.shape[1:]), BF16)
        like_copy(index).start()

    all_chunks(
        start_of, count, ZC_OUT, PLANES_OUT, ext, labels_ref,
        (wz_ref, wy_ref, wx_ref), (z_high, z_low, y_out),
        (channels, bands), acc, like, beside,
    )

    for slot in range(owner_ref.shape[0]):
        owner = owner_ref[slot]
        rank = rank_ref[slot].astype(F32)
        for scale in range(2):
            for band in range(4):
                turned[pl.ds(32 * scale + band, 8, stride=4), :] = acc[
                    pl.ds((slot // 2) * FEAT + 32 * scale + 8 * band, 8),
                    pl.ds((slot % 2) * LBL, LBL),
                ]
        for quarter in range(4):
            for part in range(4):
                send_ref[owner, quarter, part] = turned[
                    pl.ds(16 * quarter + 4 * part, 4), :
                ].astype(BF16)
            send_ref[owner, quarter, 4] = jnp.full((4, LBL), rank, F32).astype(BF16)
    for index in range(count):
        like_copy(index).wait()
    inner_copy.wait()


def sum_kernel(got_ref, out_ref):
    sources, parts = (got_ref.shape[0], got_ref.shape[1] - 1)

    def step(source, totals):
        rank = got_ref[source, parts].astype(F32)
        data = [got_ref[source, part].astype(F32) for part in range(parts)]
        return tuple(
            tuple(
                total + jnp.where(rank == float(index), block, 0.0)
                for total, block in zip(row, data)
            )
            for index, row in enumerate(totals)
        )

    zero = jnp.zeros((4, LBL), F32)
    totals = lax.fori_loop(
        0, sources, step, ((zero,) * parts,) * out_ref.shape[0], unroll=8
    )
    for index, row in enumerate(totals):
        for part, total in enumerate(row):
            out_ref[index, pl.ds(4 * part, 4)] = total


def neighbours(shard, axis, dim, width):
    size, length = (lax.axis_size(axis), shard.shape[dim])
    up = [(i, (i + 1) % size) for i in range(size)]
    down = [(j, i) for i, j in up]
    last = lax.slice_in_dim(shard, length - width, length, axis=dim)
    leading = lax.slice_in_dim(shard, 0, width, axis=dim)
    here = lax.axis_index(axis)
    ends = (here == 0, here == size - 1)
    return (lax.ppermute(last, axis, up), lax.ppermute(leading, axis, down), ends)


VMEM = pl.BlockSpec(memory_space=pltpu.VMEM)
SMEM = pl.BlockSpec(memory_space=pltpu.SMEM)


def scratch(chunk, slab_z, rows_y, width):
    rows = chunk * rows_y
    deep = rows_y + 2 * HALO
    return [
        pltpu.VMEM((slab_z + 2 * HALO, deep, width), F32),
        pltpu.VMEM((6, chunk, deep, width), BF16),
        pltpu.VMEM((6, chunk, deep, width), BF16),
        pltpu.VMEM((12, rows, width), F32),
        pltpu.VMEM((16 * rows, width), F32),
        pltpu.VMEM((4 * rows, width), F32),
    ]


def cost(share):
    return pl.CostEstimate(
        flops=int(share * 28e9), bytes_accessed=int(share * 4e6), transcendentals=int(share * 4e5)
    )


PARAMS = pltpu.CompilerParams(vmem_limit_bytes=36 * 1024 * 1024)


def inner_sums(own, labels):
    matrices = filter_matrices(ZP_IN, *labels.shape[1:])
    return pl.pallas_call(
        inner_kernel,
        out_shape=(
            jax.ShapeDtypeStruct(labels.shape, BF16),
            jax.ShapeDtypeStruct((HI * FEAT, LO), F32),
        ),
        in_specs=[VMEM] * 5,
        out_specs=(VMEM, VMEM),
        scratch_shapes=scratch(ZC_IN, *labels.shape),
        compiler_params=PARAMS,
        cost_estimate=cost(0.25),
    )(own, labels, *matrices)


def outer_sums(owners, ranks, ends, before, own, after, labels, inner, groups, quarters):
    matrices = filter_matrices(ZP_OUT, *labels.shape[1:])
    return pl.pallas_call(
        outer_kernel,
        out_shape=(
            jax.ShapeDtypeStruct(labels.shape, BF16),
            jax.ShapeDtypeStruct((groups, quarters, SEND, 4, LBL), BF16),
        ),
        in_specs=[SMEM] * 3 + [VMEM] * 9,
        out_specs=(pl.BlockSpec(memory_space=pl.ANY), VMEM),
        scratch_shapes=scratch(ZC_OUT, *labels.shape)
        + [
            pltpu.VMEM((HI * FEAT, LO), F32),
            pltpu.VMEM((FEAT, LBL), F32),
            pltpu.VMEM(labels.shape, BF16),
            pltpu.SemaphoreType.DMA((2 * HALO // ZC_OUT + 1,)),
        ],
        compiler_params=PARAMS,
        cost_estimate=cost(0.75),
    )(owners, ranks, ends, before, own, after, labels, *matrices, *inner)


def local(image, labels, brick_blocks, block_owner):
    groups = lax.axis_size("gy")
    quarters = lax.axis_size("gz")
    listed_count = brick_blocks.shape[-1]
    total_blocks = block_owner.shape[0]
    blk_dev = total_blocks // groups
    block_index = jnp.arange(total_blocks, dtype=jnp.int32)
    earlier = (block_index[None, :] < block_index[:, None]) & (
        block_owner[None, :] == block_owner[:, None]
    )
    owner_rank = jnp.sum(earlier.astype(jnp.int32), axis=1)
    listed_ids = brick_blocks.reshape(listed_count)
    listed = (listed_ids[:, None] == block_index[None, :]).astype(jnp.int32)
    owners = jnp.sum(listed * block_owner[None, :], axis=1)
    ranks = jnp.sum(listed * owner_rank[None, :], axis=1)

    left, right, (first, last) = neighbours(image, "gy", 1, HALO)
    zero = jnp.zeros((), image.dtype)
    own = jnp.concatenate(
        [jnp.where(first, zero, left), image, jnp.where(last, zero, right)], axis=1
    )
    before, after, ends = neighbours(own, "gz", 0, HALO)
    inner = inner_sums(own, labels)
    likeness, message = outer_sums(
        owners, ranks, jnp.stack(ends).astype(jnp.int32), before, own, after, labels, inner,
        groups, quarters,
    )
    message = message.reshape(groups * quarters, SEND, 4, LBL)
    got = lax.all_to_all(message, ("gy", "gz"), 0, 0, tiled=True)
    label_features = pl.pallas_call(
        sum_kernel,
        out_shape=jax.ShapeDtypeStruct((blk_dev, FEAT // quarters, LBL), F32),
        compiler_params=pltpu.CompilerParams(vmem_limit_bytes=6 * 1024 * 1024),
    )(got)
    return (likeness, label_features)


def solution(mesh):
    placed = (P("gz", "gy", None), P("gz", "gy", None), P("gz", "gy", None), P())
    return jax.shard_map(
        local,
        mesh=mesh,
        in_specs=placed,
        out_specs=(P("gz", "gy", None), P("gy", "gz", None)),
        check_vma=False,
    )
```

```python
import math

import jax
import jax.numpy as jnp
import ml_dtypes
import numpy as np
from jax import lax
from jax.experimental import pallas as pl
from jax.experimental.pallas import tpu as pltpu
from jax.sharding import PartitionSpec as P

LBL = 128
FEAT = 64
HALO = 12
ZC_IN, ZC_OUT = (8, 12)
ZP_IN, ZP_OUT = (8, 6)
PLANES_IN, PLANES_OUT = (4, 6)
SIGMAS = (2, 4)
CENTERS = (-1.5, -0.5, 0.5, 1.5)
ORDERS = ((2, 0, 0), (0, 2, 0), (0, 0, 2), (1, 1, 0), (1, 0, 1), (0, 1, 1))
HI = 8
LO = 256
SEND = 5
F32, BF16 = jnp.float32, jnp.bfloat16


def kernel_set(sigma_val):
    radius = 3 * sigma_val
    offsets = [float(step) for step in range(-radius, radius + 1)]
    smooth = [math.exp(-step * step / (2.0 * sigma_val**2)) for step in offsets]
    weight_total = sum(smooth)
    smooth = [value / weight_total for value in smooth]
    first_order = [step / sigma_val**2 * value for step, value in zip(offsets, smooth)]
    second = [
        (step * step / sigma_val**4 - 1.0 / sigma_val**2) * value
        for step, value in zip(offsets, smooth)
    ]
    return (radius, [smooth, first_order, second])


def banded(weights, radius, rows, columns, offset):
    matrix = np.zeros((rows, columns))
    for row in range(rows):
        for tap, weight in enumerate(weights):
            column = row + offset + tap - radius
            if 0 <= column < columns:
                matrix[row, column] = weight
    return matrix


def two_parts(matrix):
    high = matrix.astype(np.float32).astype(ml_dtypes.bfloat16)
    low = (matrix - high.astype(np.float64)).astype(np.float32).astype(ml_dtypes.bfloat16)
    return (high, low)


def filter_matrices(chunk, rows_y, width):
    along_z, along_y, along_x = ([], [], [])
    for sigma_val in SIGMAS:
        radius, filters = kernel_set(sigma_val)
        y_rows = []
        for order in range(3):
            z_matrix = banded(filters[order], radius, chunk, chunk + 2 * HALO, HALO)
            along_z.append(np.kron(z_matrix, np.eye(8)))
            y_rows.append(banded(filters[order], radius, rows_y, rows_y + 2 * HALO, HALO))
            x_matrix = banded(filters[order], radius, width, width, 0).T
            parts = np.concatenate(two_parts(x_matrix * (4.0 * sigma_val**3.5)), axis=1)
            along_x.append(np.concatenate([parts, parts], axis=0))
        y_matrix = np.concatenate(y_rows)
        y_matrix = np.pad(y_matrix, ((0, -y_matrix.shape[0] % 16), (0, 0)))
        high, low = two_parts(y_matrix)
        along_y.append(np.concatenate([high, high, low], axis=1))
    z_parts = np.concatenate(two_parts(np.concatenate(along_z)), axis=0)
    return (z_parts, np.stack(along_y), np.stack(along_x))


def split(value):
    high = value.astype(BF16)
    return (high, (value - high.astype(F32)).astype(BF16))


def filters_of(
    z_start, chunk, ext, wz_ref, wy_ref, wx_ref, z_high, z_low, y_out, channels, bands, like_ref
):
    rows_y, width = like_ref.shape[1:]
    deep = rows_y + 2 * HALO
    rows = chunk * rows_y
    piece = wz_ref.shape[0] // (2 * 6 * 8)
    planes = 6 * piece

    for first in range(0, chunk, piece):
        for pair in range(deep // 16):
            tiles = [
                ext[pl.ds(z_start + first, piece + 2 * HALO), pl.ds(16 * pair + 8 * half, 8), :]
                .reshape((piece + 2 * HALO) * 8, width)
                .astype(BF16)
                for half in range(2)
            ]
            out = jnp.dot(wz_ref[...], jnp.concatenate(tiles, axis=1), preferred_element_type=F32)
            out = (out[: planes * 8] + out[planes * 8 :]).reshape(planes, 8, 2 * width)
            out = jnp.concatenate([out[:, :, :width], out[:, :, width:]], axis=1)
            high, low = split(out.reshape(6, piece, 16, width))
            z_high[:, pl.ds(first, piece), pl.ds(16 * pair, 16), :] = high
            z_low[:, pl.ds(first, piece), pl.ds(16 * pair, 16), :] = low

    for scale in range(2):
        for order_z in range(3):
            for pair in range(chunk // 2):
                columns = []
                for half in range(2):
                    index = (scale * 3 + order_z, 2 * pair + half)
                    columns.append(
                        jnp.concatenate([z_high[index], z_low[index], z_high[index]], axis=0)
                    )
                deep_rows = jnp.concatenate(columns, axis=1)
                count = (3 - order_z) * rows_y
                out = jnp.dot(
                    wy_ref[scale, :count, :], deep_rows, preferred_element_type=F32
                )
                for order_y in range(3 - order_z):
                    component = [
                        i for i, o in enumerate(ORDERS) if o[1:] == (order_y, order_z)
                    ][0]
                    both = jnp.concatenate(
                        [
                            out[
                                order_y * rows_y : (order_y + 1) * rows_y,
                                half * width : (half + 1) * width,
                            ]
                            for half in range(2)
                        ],
                        axis=0,
                    )
                    for index, part in enumerate(split(both)):
                        y_out[
                            scale * 6 + component,
                            pl.ds(2 * pair * rows_y, 2 * rows_y),
                            pl.ds(index * width, width),
                        ] = part

    tubes = []
    for scale in range(2):
        hessian = [None] * 6
        for order_x in range(3):
            members = [i for i, o in enumerate(ORDERS) if o[0] == order_x]
            two = [y_out[scale * 6 + i] for i in members]
            out = jnp.dot(
                jnp.concatenate(two, axis=0),
                wx_ref[scale * 3 + order_x],
                preferred_element_type=F32,
            )
            out = out[:, :width] + out[:, width:]
            for index, member in enumerate(members):
                hessian[member] = out[index * rows : (index + 1) * rows]
        xx, yy, zz, xy, xz, yz = hessian
        trace = xx + yy + zz
        frob = xx * xx + yy * yy + zz * zz + 2.0 * (xy * xy + xz * xz + yz * yz)
        minors = 0.5 * (trace * trace - frob)
        tube = jnp.maximum(-trace, 0.0) * jnp.maximum(minors, 0.0) / (frob + 0.25)
        tubes.append(tube)
        for index, value in enumerate(hessian + [minors, tube]):
            channels[pl.ds((scale * 8 + index) * rows, rows), :] = value
    like = jnp.maximum(tubes[0], tubes[1])
    like_ref[pl.ds(z_start, chunk)] = like.reshape(chunk, rows_y, width).astype(BF16)

    volume = ext[pl.ds(z_start + HALO, chunk), pl.ds(HALO, rows_y), :].reshape(rows, width)
    for index, center in enumerate(CENTERS):
        bands[pl.ds(index * rows, rows), :] = jnp.exp(-((volume - center) ** 2))


def add_sums(z_start, chunk, planes, labels_ref, channels, bands, acc):
    rows_y, width = labels_ref.shape[1:]
    rows = chunk * rows_y
    group = planes * rows_y
    low_ids = lax.broadcasted_iota(jnp.int32, (LO, width), 0).astype(F32).astype(BF16)

    def step(part, carry):
        left, right = ([], [])
        marks = labels_ref[pl.ds(z_start + part * planes, planes)].reshape(group, width)
        mark_high = (marks >> 8).astype(F32)
        mark_low = (marks & 255).astype(F32)
        for row in range(group):
            at = part * group + row
            feats = []
            for scale in range(2):
                base = channels[pl.ds(scale * 8 * rows + at, 8, stride=rows), :]
                for band in range(4):
                    feats.append(base * bands[pl.ds(band * rows + at, 1), :])
            feats = jnp.concatenate(feats, axis=0).astype(BF16)
            high_of = jnp.broadcast_to(mark_high[row : row + 1], (FEAT, width)).astype(BF16)
            low_of = jnp.broadcast_to(mark_low[row : row + 1], (LO, width)).astype(BF16)
            zero = jnp.zeros_like(feats)
            left.append(
                jnp.concatenate(
                    [jnp.where(high_of == jnp.asarray(h, BF16), feats, zero) for h in range(HI)],
                    axis=0,
                )
            )
            right.append(
                jnp.where(low_of == low_ids, jnp.asarray(1, BF16), jnp.asarray(0, BF16))
            )
        acc[...] += lax.dot_general(
            jnp.concatenate(left, axis=1),
            jnp.concatenate(right, axis=1),
            (((1,), (1,)), ((), ())),
            preferred_element_type=F32,
        )
        return carry

    lax.fori_loop(0, chunk // planes, step, 0)


def all_chunks(
    start_of, count, chunk, planes, ext, labels_ref, weights, passes, buffers, acc, like_ref,
    beside=lambda index: None,
):
    def step(index, carry):
        z_start = start_of(index)
        filters_of(z_start, chunk, ext, *weights, *passes, *buffers, like_ref)
        beside(index)
        add_sums(z_start, chunk, planes, labels_ref, *buffers, acc)
        return carry

    lax.fori_loop(0, count, step, 0)


def inner_kernel(
    own_ref, labels_ref, wz_ref, wy_ref, wx_ref,
    like_ref, acc,
    ext, z_high, z_low, y_out, channels, bands,
):
    slab_z = labels_ref.shape[0]
    ext[pl.ds(HALO, slab_z)] = own_ref[...].astype(F32)
    acc[...] = jnp.zeros_like(acc)
    all_chunks(
        lambda index: HALO + index * ZC_IN, (slab_z - 2 * HALO) // ZC_IN, ZC_IN, PLANES_IN, ext, labels_ref,
        (wz_ref, wy_ref, wx_ref), (z_high, z_low, y_out),
        (channels, bands), acc, like_ref,
    )


def outer_kernel(
    owner_ref, rank_ref, ends_ref, before_ref, own_ref, after_ref, labels_ref, wz_ref, wy_ref,
    wx_ref, inner_like_ref, inner_acc_ref,
    like_ref, send_ref,
    ext, z_high, z_low, y_out, channels, bands, acc, turned, like, like_sems,
):
    slab_z = labels_ref.shape[0]
    ext[pl.ds(HALO, slab_z)] = own_ref[...].astype(F32)
    for end, (ref, at) in enumerate(((before_ref, 0), (after_ref, HALO + slab_z))):
        ext[pl.ds(at, HALO)] = jnp.where(ends_ref[end] != 0, 0.0, ref[...].astype(F32))
    acc[...] = inner_acc_ref[...]
    inner = pl.ds(HALO, slab_z - 2 * HALO)
    half = HALO // ZC_OUT
    count = 2 * half
    share = send_ref.shape[0] // count
    inner_copy = pltpu.make_async_copy(
        inner_like_ref.at[inner], like_ref.at[inner], like_sems.at[count]
    )
    inner_copy.start()

    def start_of(index):
        return index * ZC_OUT + jnp.where(index >= half, slab_z - 2 * HALO, 0)

    def like_copy(index):
        planes = pl.ds(start_of(index), ZC_OUT)
        return pltpu.make_async_copy(like.at[planes], like_ref.at[planes], like_sems.at[index])

    def beside(index):
        send_ref[pl.ds(index * share, share)] = jnp.zeros((share, *send_ref.shape[1:]), BF16)
        like_copy(index).start()

    all_chunks(
        start_of, count, ZC_OUT, PLANES_OUT, ext, labels_ref,
        (wz_ref, wy_ref, wx_ref), (z_high, z_low, y_out),
        (channels, bands), acc, like, beside,
    )

    for slot in range(owner_ref.shape[0]):
        owner = owner_ref[slot]
        rank = rank_ref[slot].astype(F32)
        for scale in range(2):
            for band in range(4):
                turned[pl.ds(32 * scale + band, 8, stride=4), :] = acc[
                    pl.ds((slot // 2) * FEAT + 32 * scale + 8 * band, 8),
                    pl.ds((slot % 2) * LBL, LBL),
                ]
        for quarter in range(4):
            for part in range(4):
                send_ref[owner, quarter, part] = turned[
                    pl.ds(16 * quarter + 4 * part, 4), :
                ].astype(BF16)
            send_ref[owner, quarter, 4] = jnp.full((4, LBL), rank, F32).astype(BF16)
    for index in range(count):
        like_copy(index).wait()
    inner_copy.wait()


def sum_kernel(got_ref, out_ref):
    sources, parts = (got_ref.shape[0], got_ref.shape[1] - 1)

    def step(source, totals):
        rank = got_ref[source, parts].astype(F32)
        data = [got_ref[source, part].astype(F32) for part in range(parts)]
        return tuple(
            tuple(
                total + jnp.where(rank == float(index), block, 0.0)
                for total, block in zip(row, data)
            )
            for index, row in enumerate(totals)
        )

    zero = jnp.zeros((4, LBL), F32)
    totals = lax.fori_loop(
        0, sources, step, ((zero,) * parts,) * out_ref.shape[0], unroll=8
    )
    for index, row in enumerate(totals):
        for part, total in enumerate(row):
            out_ref[index, pl.ds(4 * part, 4)] = total


def neighbours(shard, axis, dim, width):
    size, length = (lax.axis_size(axis), shard.shape[dim])
    up = [(i, (i + 1) % size) for i in range(size)]
    down = [(j, i) for i, j in up]
    last = lax.slice_in_dim(shard, length - width, length, axis=dim)
    leading = lax.slice_in_dim(shard, 0, width, axis=dim)
    here = lax.axis_index(axis)
    ends = (here == 0, here == size - 1)
    return (lax.ppermute(last, axis, up), lax.ppermute(leading, axis, down), ends)


VMEM = pl.BlockSpec(memory_space=pltpu.VMEM)
SMEM = pl.BlockSpec(memory_space=pltpu.SMEM)


def scratch(chunk, slab_z, rows_y, width):
    rows = chunk * rows_y
    deep = rows_y + 2 * HALO
    return [
        pltpu.VMEM((slab_z + 2 * HALO, deep, width), F32),
        pltpu.VMEM((6, chunk, deep, width), BF16),
        pltpu.VMEM((6, chunk, deep, width), BF16),
        pltpu.VMEM((12, rows, 2 * width), BF16),
        pltpu.VMEM((16 * rows, width), F32),
        pltpu.VMEM((4 * rows, width), F32),
    ]


def cost(share):
    return pl.CostEstimate(
        flops=int(share * 28e9), bytes_accessed=int(share * 4e6), transcendentals=int(share * 4e5)
    )


PARAMS = pltpu.CompilerParams(vmem_limit_bytes=36 * 1024 * 1024)


def inner_sums(own, labels):
    matrices = filter_matrices(ZP_IN, *labels.shape[1:])
    return pl.pallas_call(
        inner_kernel,
        out_shape=(
            jax.ShapeDtypeStruct(labels.shape, BF16),
            jax.ShapeDtypeStruct((HI * FEAT, LO), F32),
        ),
        in_specs=[VMEM] * 5,
        out_specs=(VMEM, VMEM),
        scratch_shapes=scratch(ZC_IN, *labels.shape),
        compiler_params=PARAMS,
        cost_estimate=cost(0.25),
    )(own, labels, *matrices)


def outer_sums(owners, ranks, ends, before, own, after, labels, inner, groups, quarters):
    matrices = filter_matrices(ZP_OUT, *labels.shape[1:])
    return pl.pallas_call(
        outer_kernel,
        out_shape=(
            jax.ShapeDtypeStruct(labels.shape, BF16),
            jax.ShapeDtypeStruct((groups, quarters, SEND, 4, LBL), BF16),
        ),
        in_specs=[SMEM] * 3 + [VMEM] * 9,
        out_specs=(pl.BlockSpec(memory_space=pl.ANY), VMEM),
        scratch_shapes=scratch(ZC_OUT, *labels.shape)
        + [
            pltpu.VMEM((HI * FEAT, LO), F32),
            pltpu.VMEM((FEAT, LBL), F32),
            pltpu.VMEM(labels.shape, BF16),
            pltpu.SemaphoreType.DMA((2 * HALO // ZC_OUT + 1,)),
        ],
        compiler_params=PARAMS,
        cost_estimate=cost(0.75),
    )(owners, ranks, ends, before, own, after, labels, *matrices, *inner)


def local(image, labels, brick_blocks, block_owner):
    groups = lax.axis_size("gy")
    quarters = lax.axis_size("gz")
    listed_count = brick_blocks.shape[-1]
    total_blocks = block_owner.shape[0]
    blk_dev = total_blocks // groups
    block_index = jnp.arange(total_blocks, dtype=jnp.int32)
    earlier = (block_index[None, :] < block_index[:, None]) & (
        block_owner[None, :] == block_owner[:, None]
    )
    owner_rank = jnp.sum(earlier.astype(jnp.int32), axis=1)
    listed_ids = brick_blocks.reshape(listed_count)
    listed = (listed_ids[:, None] == block_index[None, :]).astype(jnp.int32)
    owners = jnp.sum(listed * block_owner[None, :], axis=1)
    ranks = jnp.sum(listed * owner_rank[None, :], axis=1)

    left, right, (first, last) = neighbours(image, "gy", 1, HALO)
    zero = jnp.zeros((), image.dtype)
    own = jnp.concatenate(
        [jnp.where(first, zero, left), image, jnp.where(last, zero, right)], axis=1
    )
    before, after, ends = neighbours(own, "gz", 0, HALO)
    inner = inner_sums(own, labels)
    likeness, message = outer_sums(
        owners, ranks, jnp.stack(ends).astype(jnp.int32), before, own, after, labels, inner,
        groups, quarters,
    )
    message = message.reshape(groups * quarters, SEND, 4, LBL)
    got = lax.all_to_all(message, ("gy", "gz"), 0, 0, tiled=True)
    label_features = pl.pallas_call(
        sum_kernel,
        out_shape=jax.ShapeDtypeStruct((blk_dev, FEAT // quarters, LBL), F32),
        compiler_params=pltpu.CompilerParams(vmem_limit_bytes=6 * 1024 * 1024),
    )(got)
    return (likeness, label_features)


def solution(mesh):
    placed = (P("gz", "gy", None), P("gz", "gy", None), P("gz", "gy", None), P())
    return jax.shard_map(
        local,
        mesh=mesh,
        in_specs=placed,
        out_specs=(P("gz", "gy", None), P("gy", "gz", None)),
        check_vma=False,
    )
```
